32 devices in a mesh: batch: 8 (over z, y), mp: 4 (over x, core).
Axes of the slice: x: 2, y: 2, z: 4, core: 2. Of those that a mesh axis runs over, the one named last changes fastest.
Arguments:
- tokens: bfloat16 [32, 2048, 768], P(('batch', 'mp')), may hold values from -6 to 6
- key_mask: int32 [32, 2048], P(('batch', 'mp')), may hold values 0 or 1
- lengths: int32 [32], P(('batch', 'mp')), may hold values from 1024 to 2048, as said below
- routed: int32 [32, 256], P(('batch', 'mp')), may hold values from 0 to 2047, as said below
- w_router: bfloat16 [768], replicated, may hold values from -0.21875 to 0.21875
- gain_one: bfloat16 [768], replicated, may hold values from 0.25 to 1.75
- gain_two: bfloat16 [768], replicated, may hold values from 0.25 to 1.75
- w_qkv: bfloat16 [768, 2304], replicated, may hold values from -0.21875 to 0.21875
- w_out: bfloat16 [768, 768], replicated, may hold values from -0.625 to 0.625
- w_up: bfloat16 [768, 3072], P(None, 'mp'), may hold values from -0.21875 to 0.21875
- w_down: bfloat16 [3072, 768], P('mp'), may hold values from -0.109375 to 0.109375
- cotangent: bfloat16 [32, 2048, 768], P(('batch', 'mp')), may hold values from -6 to 6
Outputs:
- block_out: bfloat16 [32, 2048, 768], P(('batch', 'mp'))
- grad_tokens: bfloat16 [32, 2048, 768], P(('batch', 'mp'))
- grad_router: float32 [768], P('batch')
- grad_gain_one: float32 [768], P('batch')
- grad_gain_two: float32 [768], P('batch')
- grad_qkv: float32 [768, 2304], P('batch')
- grad_out: float32 [768, 768], P('batch')
- grad_up: float32 [768, 3072], P('batch', 'mp')
- grad_down: float32 [3072, 768], P('mp', 'batch')
The draws below stay inside these ranges and needn't reach their ends.
Inputs may be any that keep to these rules, and one draw needn't show every extreme that they name: Each length is a multiple of 8. For every sequence s with s // 4 even, lengths[s] + lengths[s + 4] = 3072. One sequence, drawn from the seed, has 2048 and its partner 2048 // 2. `routed`: row s holds in its first lengths[s] // 8 entries distinct positions below lengths[s] in rising order, the last of them lengths[s] - 1; its other entries are 0.
All inputs are finite; a program needn't handle non-finite values. No bound on the sum of `key_mask` on one device may be relied on, other than what follows from the above.
Results may differ from the reference program's by a relative error of at most 0.015.
Values may be sent and summed in bfloat16 or wider, within the bound.
A program may use at most 192 MiB of HBM per device.

```python
import jax
import jax.numpy as jnp
from jax import lax

D = 768
HEADS = 12
HDIM = 64
FF = 3072
SEQ_LEN = 2048
KMAX = 256
SEQS = 32
N_MP = 4


def lengths_of(key):
    key = jax.random.fold_in(key, 11)
    key_units, key_full = jax.random.split(key, 2)
    lead_draw = jax.random.randint(key_units, (SEQS,), KMAX // 2, KMAX + 1)
    seq_index = jnp.arange(SEQS)
    batch_index = seq_index // N_MP
    odd_batch = batch_index % 2
    lead_index = seq_index - odd_batch * N_MP
    full_index = jax.random.randint(key_full, (), 0, SEQS)
    full_lead = full_index - full_index // N_MP % 2 * N_MP
    lead_units = jnp.take(lead_draw, lead_index)
    lead_units = jnp.where(lead_index == full_lead, KMAX, lead_units)
    length_units = jnp.where(odd_batch == 0, lead_units, 3 * KMAX // 2 - lead_units)
    return (length_units * 8).astype(jnp.int32)


def draw_lengths(key, part):
    shared = lengths_of(key)
    return shared


def draw_routed(key, part):
    length = lengths_of(key)
    key = jax.random.fold_in(key, 5)
    live_count = length // 8
    seq_keys = jax.random.split(key, SEQS)
    shuffled = jax.vmap(lambda one_key: jax.random.permutation(one_key, SEQ_LEN))(seq_keys).astype(jnp.int32)
    position = jnp.arange(SEQ_LEN, dtype=jnp.int32)[None, :]
    priority = jnp.where(position < length[:, None], shuffled + 1, SEQ_LEN + 1 + position)
    priority = jnp.where(position == length[:, None] - 1, 0, priority)
    ranked = jnp.argsort(priority, axis=1, stable=True)[:, :KMAX].astype(jnp.int32)
    slot_ids = jnp.arange(KMAX, dtype=jnp.int32)[None, :]
    chosen = jnp.where(slot_ids < live_count[:, None], ranked, SEQ_LEN)
    chosen = jnp.sort(chosen, axis=1)
    return jnp.where(slot_ids < live_count[:, None], chosen, 0).astype(jnp.int32)


def place_ends(values, own_key, least, largest):
    dims = values.shape
    index_at = [jax.random.randint(jax.random.fold_in(own_key, axis), (), 0, dims[axis]) for axis in range(len(dims))]
    values = values.at[tuple(index_at)].set(least)
    longest = dims.index(max(dims))
    index_at[longest] = (index_at[longest] + 1) % dims[longest]
    return values.at[tuple(index_at)].set(largest)


def level_of(own_key, extent, cuts, smallest, high):
    loudness, own = 1.0, jax.random.fold_in(own_key, 6)
    for axis_at, shards_of in cuts:
        steps = jnp.exp(jax.random.uniform(jax.random.fold_in(own, axis_at), (shards_of,), jnp.float32, smallest / len(cuts), high / len(cuts)))
        loudness = loudness * jnp.repeat(steps, extent[axis_at] // shards_of).reshape([-1 if axis == axis_at else 1 for axis in range(len(extent))])
    return loudness


def normal_values(stream_key, shape, spread, limit, cuts=(), held_as=jnp.bfloat16):
    values = spread * jax.random.normal(stream_key, shape, jnp.float32)
    if cuts:
        values = values * level_of(stream_key, shape, cuts, -0.22, 0.18)
    return jnp.clip(values, -limit, limit).astype(held_as)


def setup_inputs(seed: int = 0) -> dict:
    arg_keys = jax.random.split(jax.random.key(seed), 13)
    tokens = normal_values(arg_keys[0], (SEQS, SEQ_LEN, D), 1.0, 6.0, ((0, 32),))
    key_mask = place_ends((jax.random.randint(arg_keys[1], (SEQS, SEQ_LEN), 0, 8) < 7).astype(jnp.int32), jax.random.fold_in(arg_keys[1], 1), 0, 1)
    lengths = draw_lengths(jax.random.fold_in(arg_keys[12], 71), 0)
    routed = draw_routed(jax.random.fold_in(arg_keys[12], 71), 0)
    w_router = normal_values(arg_keys[4], (D,), D ** -0.5, 0.21875)
    gain_one = jnp.clip(1.0 + 0.15 * jax.random.normal(arg_keys[5], (D,), jnp.float32), 0.25, 1.75).astype(jnp.bfloat16)
    gain_two = jnp.clip(1.0 + 0.15 * jax.random.normal(arg_keys[6], (D,), jnp.float32), 0.25, 1.75).astype(jnp.bfloat16)
    w_qkv = normal_values(arg_keys[7], (D, 3 * D), D ** -0.5, 0.21875)
    w_out = normal_values(arg_keys[8], (D, D), (D // 8) ** -0.5, 0.625)
    w_up = normal_values(arg_keys[9], (D, FF), D ** -0.5, 0.21875, ((1, 4),))
    w_down = normal_values(arg_keys[10], (FF, D), FF ** -0.5, 0.109375, ((0, 4),))
    cotangent = normal_values(arg_keys[11], (SEQS, SEQ_LEN, D), 1.0, 6.0, ((0, 32),))
    return {"tokens": tokens, "key_mask": key_mask, "lengths": lengths, "routed": routed, "w_router": w_router, "gain_one": gain_one, "gain_two": gain_two, "w_qkv": w_qkv, "w_out": w_out, "w_up": w_up, "w_down": w_down, "cotangent": cotangent}


EPSILON = 1e-06

@jax.custom_vjp
def low(v):
    return lax.optimization_barrier(v.astype(jnp.bfloat16)).astype(jnp.float32)

@jax.custom_vjp
def low_back(v):
    return v

def low_keep(v):
    return (low(v), None)

def low_pass(kept, grad):
    return (grad,)

def back_keep(v):
    return (v, None)

def back_low(kept, grad):
    return (low(grad),)
low.defvjp(low_keep, low_pass)
low_back.defvjp(back_keep, back_low)

def rms_scale(v, g):
    return v * lax.rsqrt(lax.optimization_barrier(jnp.mean(v * v, axis=-1, keepdims=True)) + EPSILON) * g

def masked_probs(scores, allowed):
    shifted = jnp.where(allowed, scores, -1e+30)
    shifted = shifted - lax.optimization_barrier(jnp.max(shifted, axis=-1, keepdims=True))
    exp_scores = jnp.exp(shifted)
    return exp_scores / lax.optimization_barrier(jnp.sum(exp_scores, axis=-1, keepdims=True))

def one_sequence(seq_tokens, mask_row, length, select_ids, w_router, gain_one, gain_two, w_qkv, w_out, w_up, w_down):
    highest = lax.Precision.HIGHEST
    routed_max = select_ids.shape[0]
    slot_ids = jnp.arange(routed_max, dtype=jnp.int32)
    live_mask = (slot_ids < length // 8).astype(seq_tokens.dtype)
    picked = jnp.take(seq_tokens, select_ids, axis=0)
    gate_rate = jax.nn.sigmoid(jnp.dot(picked, w_router, precision=highest))
    normed_one = low(rms_scale(picked, gain_one))
    qkv_rows = low_back(low(jnp.dot(normed_one, w_qkv, precision=highest)))
    queries = qkv_rows[:, :D].reshape(routed_max, HEADS, HDIM)
    key_heads = qkv_rows[:, D:2 * D].reshape(routed_max, HEADS, HDIM)
    values = qkv_rows[:, 2 * D:].reshape(routed_max, HEADS, HDIM)
    scores = low_back(jnp.einsum('qhd,khd->hqk', queries, key_heads, precision=highest) * HDIM ** (-0.5))
    key_open = jnp.take(mask_row, select_ids) == 1
    allowed = (slot_ids[None, :] < slot_ids[:, None]) & key_open[None, :] | (slot_ids[None, :] == slot_ids[:, None])
    attn_probs = low(masked_probs(scores, allowed[None]))
    mixed = low_back(low(jnp.einsum('hqk,khd->qhd', attn_probs, values, precision=highest).reshape(routed_max, D)))
    attended = low_back(jnp.dot(mixed, w_out, precision=highest))
    residual = picked + attended
    second = low_back(low(rms_scale(residual, gain_two)))
    pre_act = low_back(jnp.dot(second, w_up, precision=highest))
    activation = low(jax.nn.gelu(pre_act))
    mlp_out = low_back(low(jnp.dot(activation, w_down, precision=highest)))
    branch = attended + mlp_out
    return seq_tokens.at[select_ids].add((live_mask * gate_rate)[:, None] * branch)

def reference(tokens, key_mask, lengths, routed, w_router, gain_one, gain_two, w_qkv, w_out, w_up, w_down, cotangent):
    weights = tuple((w.astype(jnp.float32) for w in (w_router, gain_one, gain_two, w_qkv, w_out, w_up, w_down)))

    def seq_step(totals, inputs):
        seq_tokens, mask_row, length, select_ids, seq_cot = inputs

        def seq_forward(float_tokens, *params):
            return one_sequence(float_tokens, mask_row, length, select_ids, *params)
        result, backward = jax.vjp(seq_forward, seq_tokens.astype(jnp.float32), *weights)
        gradients = backward(seq_cot.astype(jnp.float32))
        totals = tuple((a + b for a, b in zip(totals, gradients[1:])))
        return (totals, (result.astype(jnp.bfloat16), gradients[0].astype(jnp.bfloat16)))
    zero_grads = tuple((jnp.zeros(w.shape, jnp.float32) for w in weights))
    totals, (block_out, grad_tokens) = lax.scan(seq_step, zero_grads, (tokens, key_mask, lengths, routed, cotangent))
    return (block_out, grad_tokens, totals[0], totals[1], totals[2], totals[3], totals[4], totals[5], totals[6])
```

```python
import functools
import types

import jax
import jax.numpy as jnp
from jax import lax
from jax.experimental import pallas as pl
from jax.experimental.pallas import tpu as pltpu
from jax.sharding import PartitionSpec as P

HEADS = 12
EPSILON = 1e-06
LOW = jnp.bfloat16
F32 = jnp.float32
MESH = pl.DeviceIdType.MESH
VMEM_BYTES = 60 * 2**20
STAGES = 3


def mm(a, b, along_a=1, along_b=0):
    return lax.dot_general(a, b, (((along_a,), (along_b,)), ((), ())), preferred_element_type=F32)


def norm_rate(v):
    return lax.rsqrt(jnp.mean(v * v, axis=1, keepdims=True) + EPSILON)


def gelu_and_slope(v):
    c = 0.7978845608028654
    square = v * v
    t = jnp.tanh(v * (c + (c * 0.044715) * square))
    half = 0.5 + 0.5 * t
    slope = half + (0.5 * v) * (1.0 - t * t) * (c + (c * 3 * 0.044715) * square)
    return v * half, slope


def iota(shape, dim):
    return lax.broadcasted_iota(jnp.int32, shape, dim)


class Sizes:
    def __init__(self, rows, width, slots, hidden, batch):
        self.rows, self.width, self.slots, self.hidden, self.batch = rows, width, slots, hidden, batch
        self.block = width // batch
        self.folds = batch == 8 and self.block % 16 == 0
        self.part = width // STAGES


def scratch_of(s):
    n, d, f, c = s.slots, s.width, s.hidden, s.part
    tree = (2, 2, 2, s.block) if s.folds else (d,)
    found = dict(
        tok=pltpu.VMEM((s.rows, d), LOW),
        cot=pltpu.VMEM((s.rows, d), LOW),
        wqkv=pltpu.VMEM((d, 3 * d), LOW),
        wout=pltpu.VMEM((d, d), LOW),
        wup=pltpu.VMEM((2, d, f), LOW),
        wdn=pltpu.VMEM((2, f, d), LOW),
        pick=pltpu.VMEM((n, s.rows), LOW),
        picked=pltpu.VMEM((n, d), F32),
        cotr=pltpu.VMEM((n, d), LOW),
        first=pltpu.VMEM((n, d), LOW),
        qkv=pltpu.VMEM((n, 3 * d), LOW),
        bias=pltpu.VMEM((n, n), F32),
        probs=pltpu.VMEM((HEADS, n, n), LOW),
        mixed=pltpu.VMEM((n, d), LOW),
        attended=pltpu.VMEM((n, d), F32),
        resid=pltpu.VMEM((n, d), F32),
        sec=pltpu.VMEM((2, n, d), LOW),
        gm=pltpu.VMEM((2, n, d), LOW),
        act=pltpu.VMEM((2, 2 * n, f), LOW),
        gpre=pltpu.VMEM((2, 2 * n, f), LOW),
        gs_own=pltpu.VMEM((n, d), F32),
        mo_own=pltpu.VMEM((n, d), F32),
        gs_out=pltpu.VMEM((n, d), LOW),
        mo_out=pltpu.VMEM((n, d), LOW),
        gs_in=pltpu.VMEM((n, d), LOW),
        mo_in=pltpu.VMEM((n, d), LOW),
        gres=pltpu.VMEM((n, d), F32),
        gatt=pltpu.VMEM((n, d), LOW),
        gmix=pltpu.VMEM((n, d), LOW),
        dqkv=pltpu.VMEM((n, 3 * d), LOW),
        core_out=pltpu.VMEM((2, *tree, f), LOW),
        core_in=pltpu.VMEM((2, *tree, f), LOW),
        att=pltpu.VMEM((STAGES, 2, 2, *tree, c), LOW),
        att_core=pltpu.VMEM((STAGES, 2, *tree, c), LOW),
        att_x=pltpu.VMEM((STAGES, *tree, c), LOW),
        vec=pltpu.VMEM((6, 8, d), F32),
        vec_in=pltpu.VMEM((5, 8, d), F32),
        send_sem=pltpu.SemaphoreType.DMA((80,)),
        recv_sem=pltpu.SemaphoreType.DMA((80,)),
        local_sem=pltpu.SemaphoreType.DMA((8,)),
    )
    if s.folds:
        found |= dict(
            m0=pltpu.VMEM((2, 2, 2, s.block, f), LOW),
            m1=pltpu.VMEM((2, 2, s.block, f), LOW),
            m2=pltpu.VMEM((2, s.block, f), LOW),
            a0=pltpu.VMEM((STAGES, 2, 2, s.block, c), LOW),
            a1=pltpu.VMEM((STAGES, 2, s.block, c), LOW),
            a2=pltpu.VMEM((STAGES, s.block, c), LOW),
            ag=pltpu.VMEM((4, STAGES, s.block, c), LOW),
        )
    return found


def layer_kernel(s, names, *refs):
    ins, outs, scratch = refs[:12], refs[12:17], refs[17:]
    tokens, cotangent, key_mask, lengths, routed, w_router, gain_one, gain_two, w_qkv, w_out, w_up, w_down = ins
    upd_out, upd_tok, o_mlp, o_att, o_vec = outs
    v = types.SimpleNamespace(**dict(zip(names, scratch, strict=True)))
    n, d, f, c = s.slots, s.width, s.hidden, s.part
    half_rows = n // 2

    b, m = lax.axis_index("batch"), lax.axis_index("mp")
    lo, hi = m % 2, m // 2
    peer_lo, peer_hi, peer_far = (b, m + 1 - 2 * lo), (b, m + 2 - 4 * hi), (b, 3 - m)
    peers = [peer_lo, peer_hi, peer_far]
    if s.folds:
        y, zl, zh = b % 2, (b // 2) % 2, b // 4
        peer_y, peer_zl, peer_zh = (b + 1 - 2 * y, m), (b + 2 - 4 * zl, m), (b + 4 - 8 * zh, m)
        peers += [peer_y, peer_zl, peer_zh]

    barrier = pltpu.get_barrier_semaphore()
    for peer in peers:
        pl.semaphore_signal(barrier, inc=1, device_id=peer, device_id_type=MESH)

    sent = []

    def send(src, dst, peer):
        at = len(sent)
        copy = pltpu.make_async_remote_copy(
            src_ref=src,
            dst_ref=dst,
            send_sem=v.send_sem.at[at],
            recv_sem=v.recv_sem.at[at],
            device_id=peer,
            device_id_type=MESH,
        )
        copy.start()
        sent.append(copy)
        return copy

    fetches = []
    for src, dst in (
        (tokens.at[0], v.tok),
        (cotangent.at[0], v.cot),
        (w_qkv, v.wqkv),
        (w_out, v.wout),
        (w_up, v.wup.at[0]),
        (w_down, v.wdn.at[0]),
    ):
        fetches.append(pltpu.make_async_copy(src, dst, v.local_sem.at[len(fetches)]))
        fetches[-1].start()
    got_tok, got_cot, got_qkv, got_out, got_up, got_down = fetches

    live_count = lengths[0] // 8
    wanted = jnp.where(iota((1, n), 1) < live_count, routed[...], -1).astype(F32)
    on_diagonal = iota((n, n), 0) == iota((n, n), 1)
    wanted_column = jnp.sum(jnp.where(on_diagonal, wanted, 0.0), axis=1, keepdims=True).astype(jnp.int32)
    live = jnp.where(iota((n, 1), 0) < live_count, 1.0, 0.0)
    v.pick[...] = jnp.where(iota((n, s.rows), 1) == wanted_column, 1.0, 0.0).astype(LOW)

    got_tok.wait()
    picked = mm(v.pick[...], v.tok[...])
    v.picked[...] = picked
    router_row = w_router[...].astype(F32)
    one_row = gain_one[...].astype(F32)
    two_row = gain_two[...].astype(F32)
    gate_rate = 1.0 / (1.0 + jnp.exp(-jnp.sum(picked * router_row, axis=1, keepdims=True)))
    route_gain = live * gate_rate
    rate_one = norm_rate(picked)
    v.first[...] = (picked * rate_one * one_row).astype(LOW)

    got_cot.wait()
    cot_rows = mm(v.pick[...], v.cot[...])
    v.cotr[...] = cot_rows.astype(LOW)
    v.gm[0] = (route_gain * cot_rows).astype(LOW)

    pl.semaphore_wait(barrier, len(peers))
    sent_gm = send(v.gm.at[0], v.gm.at[1], peer_hi)
    sent_up = send(w_up, v.wup.at[1], peer_lo)
    sent_down = send(w_down, v.wdn.at[1], peer_lo)

    got_qkv.wait()
    for at in range(3 * STAGES):
        cols = slice(at * c, at * c + c)
        v.qkv[:, cols] = mm(v.first[...], v.wqkv[:, cols]).astype(LOW)

    mask_rows = jnp.broadcast_to(key_mask[...].astype(F32), (8, s.rows)).astype(LOW)
    key_open = mm(mask_rows, v.pick[...], 1, 1)[0:1] > 0.5
    earlier = iota((n, n), 1) < iota((n, n), 0)
    v.bias[...] = jnp.where((earlier & key_open) | on_diagonal, 0.0, -1e30)

    pair = 2 * (d // HEADS)
    lane = iota((n, pair), 1)
    side = [lane < pair // 2, lane >= pair // 2]

    def only(x, at):
        return jnp.where(side[at], x.astype(F32), 0.0).astype(LOW)

    def attend(p, _):
        at = pl.multiple_of(p * pair, pair)
        q, k, val = (v.qkv[:, pl.ds(pl.multiple_of(g * d + at, pair), pair)] for g in range(3))
        q = (q.astype(F32) * (d // HEADS) ** -0.5).astype(LOW)
        total = 0.0
        for h in range(2):
            scores = mm(only(q, h), k, 1, 1) + v.bias[...]
            powers = jnp.exp(scores - jnp.max(scores, axis=1, keepdims=True))
            probs = (powers * (1.0 / jnp.sum(powers, axis=1, keepdims=True))).astype(LOW)
            v.probs[2 * p + h] = probs
            total = total + mm(probs, only(val, h))
        v.mixed[:, pl.ds(at, pair)] = total.astype(LOW)
        return 0

    lax.fori_loop(0, HEADS // 2, attend, 0)

    got_out.wait()
    sent_sec = []
    for at in range(2):
        rows = slice(at * half_rows, (at + 1) * half_rows)
        attended = mm(v.mixed[rows], v.wout[...])
        v.attended[rows] = attended
        resid = v.picked[rows] + attended
        v.resid[rows] = resid
        v.sec[0, rows] = (resid * norm_rate(resid) * two_row).astype(LOW)
        sent_sec.append(send(v.sec.at[0, pl.ds(at * half_rows, half_rows)], v.sec.at[1, pl.ds(at * half_rows, half_rows)], peer_hi))

    got_up.wait()
    got_down.wait()

    def feed(j, start, count):
        x, g = v.sec[j, start : start + count], v.gm[j, start : start + count]
        gs, mo = 0.0, 0.0
        for w in range(2):
            rows = slice(j * n + start, j * n + start + count)
            act, slope = gelu_and_slope(mm(x, v.wup[w]))
            act = act.astype(LOW)
            v.act[w, rows] = act
            gpre = (mm(g, v.wdn[w], 1, 1) * slope).astype(LOW)
            v.gpre[w, rows] = gpre
            gs = gs + mm(gpre, v.wup[w], 1, 1)
            mo = mo + mm(act, v.wdn[w])
        return gs, mo

    sent_up.wait_recv()
    sent_down.wait_recv()
    for at in range(2):
        rows = slice(at * half_rows, (at + 1) * half_rows)
        v.gs_own[rows], v.mo_own[rows] = feed(0, at * half_rows, half_rows)

    sent_gm.wait_recv()
    sent_gs, sent_mo = [], []
    for at in range(2):
        rows = slice(at * half_rows, (at + 1) * half_rows)
        there = pl.ds(at * half_rows, half_rows)
        sent_sec[at].wait_recv()
        gs, mo = feed(1, at * half_rows, half_rows)
        v.gs_out[rows] = gs.astype(LOW)
        sent_gs.append(send(v.gs_out.at[there], v.gs_in.at[there], peer_hi))
        v.mo_out[rows] = mo.astype(LOW)
        sent_mo.append(send(v.mo_out.at[there], v.mo_in.at[there], peer_hi))

    def weight_grad(kind, w):
        left, right = (v.sec, v.gpre) if kind == 0 else (v.gm, v.act)
        return mm(left[...].reshape(2 * n, d), right[w], 0, 0)

    sent_core = []
    for kind in range(2):
        v.core_out[kind] = weight_grad(kind, 1).astype(LOW).reshape(v.core_out.shape[1:])
        sent_core.append(send(v.core_out.at[kind], v.core_in.at[kind], peer_lo))

    class Fold:
        def __init__(self, table, r0, r1, r2):
            self.table, self.r0, self.r1, self.r2 = table, r0, r1, r2

        def start_y(self):
            self.going = [send(self.table.at[at, :, 1 - y], self.r0.at[at], peer_y) for at in range(2)]

        def end_y(self):
            for copy in self.going:
                copy.wait_recv()
            for i in range(2):
                for j in range(2):
                    self.r0[i, j] = (self.r0[i, j].astype(F32) + self.table[i, j, y].astype(F32)).astype(LOW)
            self.going = [send(self.r0.at[:, 1 - zl], self.r1, peer_zl)]

        def end_zl(self):
            self.going[0].wait_recv()
            for i in range(2):
                self.r1[i] = (self.r1[i].astype(F32) + self.r0[i, zl].astype(F32)).astype(LOW)
            self.going = [send(self.r1.at[1 - zh], self.r2, peer_zh)]

        def end_zh(self):
            self.going[0].wait_recv()
            return self.r2[...].astype(F32) + self.r1[zh].astype(F32)

    mlp_folds = []
    for kind in range(2):
        own = weight_grad(kind, 0).reshape(v.core_in.shape[1:])
        sent_core[kind].wait_recv()
        v.core_in[kind] = (v.core_in[kind].astype(F32) + own).astype(LOW)
        if s.folds:
            fold = Fold(v.core_in.at[kind], v.m0.at[kind], v.m1.at[kind], v.m2.at[kind])
            fold.start_y()
            mlp_folds.append(fold)
        else:
            o_mlp[kind] = v.core_in[kind]

    gain_two_sum = 0.0
    for at in range(2):
        rows = slice(at * half_rows, (at + 1) * half_rows)
        sent_gs[at].wait_recv()
        gs = (v.gs_own[rows] + v.gs_in[rows].astype(F32)).astype(LOW).astype(F32)
        resid = v.resid[rows]
        rate = norm_rate(resid)
        gain_two_sum = gain_two_sum + jnp.sum(gs * (resid * rate), axis=0, keepdims=True)
        scaled = gs * two_row
        gres = rate * scaled - resid * (rate * rate * rate * jnp.mean(scaled * resid, axis=1, keepdims=True))
        v.gres[rows] = gres
        gatt = (route_gain[rows] * v.cotr[rows].astype(F32) + gres).astype(LOW)
        v.gatt[rows] = gatt
        v.gmix[rows] = mm(gatt, v.wout[...], 1, 1).astype(LOW)

    def attend_back(p, _):
        at = pl.multiple_of(p * pair, pair)
        where = [pl.ds(pl.multiple_of(g * d + at, pair), pair) for g in range(3)]
        q, k, val = (v.qkv[:, cols] for cols in where)
        gmix = v.gmix[:, pl.ds(at, pair)]
        gq, gk, gv = 0.0, 0.0, 0.0
        for h in range(2):
            probs = v.probs[2 * p + h]
            gmix_h = only(gmix, h)
            gprobs = mm(gmix_h, val, 1, 1)
            wide = probs.astype(F32)
            product = gprobs * wide
            gscores = product - wide * jnp.sum(product, axis=1, keepdims=True)
            gscores = (gscores * (d // HEADS) ** -0.5).astype(LOW)
            gq = gq + mm(gscores, only(k, h))
            gk = gk + mm(gscores, only(q, h), 0, 0)
            gv = gv + mm(probs, gmix_h, 0, 0)
        for cols, grad in zip(where, (gq, gk, gv), strict=True):
            v.dqkv[:, cols] = grad.astype(LOW)
        return 0

    att_core, att_x, att_folds = [], [], []

    def end_core(t):
        att_core[t].wait_recv()
        for i in range(2):
            v.att_core[t, i] = (v.att_core[t, i].astype(F32) + v.att[t, i, lo].astype(F32)).astype(LOW)
        att_x.append(send(v.att_core.at[t, 1 - hi], v.att_x.at[t], peer_hi))

    def end_x(t):
        att_x[t].wait_recv()
        v.att_x[t] = (v.att_x[t].astype(F32) + v.att_core[t, hi].astype(F32)).astype(LOW)
        if s.folds:
            fold = Fold(v.att_x.at[t], v.a0.at[t], v.a1.at[t], v.a2.at[t])
            fold.start_y()
            att_folds.append(fold)
        else:
            o_att[t] = v.att_x[t]

    for t in range(STAGES):
        lax.fori_loop(t * HEADS // 2 // STAGES, (t + 1) * HEADS // 2 // STAGES, attend_back, 0)
        for g in range(4):
            if g < 3:
                left, right = v.first[...], v.dqkv[:, g * d + t * c : g * d + t * c + c]
            else:
                left, right = v.mixed[...], v.gatt[:, t * c : t * c + c]
            v.att[t, g // 2, g % 2] = mm(left, right, 0, 0).astype(LOW).reshape(v.att.shape[3:])
        att_core.append(send(v.att.at[t, :, 1 - lo], v.att_core.at[t], peer_lo))
        if t > 0:
            end_core(t - 1)
        if s.folds and t > 0:
            mlp_folds[t - 1].end_y()
    end_core(STAGES - 1)

    gfirst = mm(v.dqkv[...], v.wqkv[...], 1, 1)
    picked = v.picked[...]
    gain_one_sum = jnp.sum(gfirst * (picked * rate_one), axis=0, keepdims=True)
    scaled = gfirst * one_row
    gnorm = rate_one * scaled - picked * (rate_one * rate_one * rate_one * jnp.mean(scaled * picked, axis=1, keepdims=True))
    for copy in sent_mo:
        copy.wait_recv()
    branch = v.attended[...] + (v.mo_own[...] + v.mo_in[...].astype(F32)).astype(LOW).astype(F32)
    grate = live * jnp.sum(v.cotr[...].astype(F32) * branch, axis=1, keepdims=True)
    glogit = grate * gate_rate * (1.0 - gate_rate)
    router_sum = jnp.sum(glogit * picked, axis=0, keepdims=True)
    upd_out[...] = (route_gain * branch).astype(LOW)
    upd_tok[...] = (live * (gnorm + v.gres[...] + glogit * router_row)).astype(LOW)

    row = iota((8, d), 0)
    v.vec[0] = jnp.where(row == 0, router_sum, jnp.where(row == 1, gain_one_sum, jnp.where(row == 2, gain_two_sum, 0.0)))
    vec_peers = [peer_lo, peer_hi] + ([peer_y, peer_zl, peer_zh] if s.folds else [])
    vec_going = []

    def vec_step():
        at = len(vec_going)
        if at:
            vec_going[-1].wait_recv()
            v.vec[at] = v.vec[at - 1] + v.vec_in[at - 1]
        if at < len(vec_peers):
            vec_going.append(send(v.vec.at[at], v.vec_in.at[at], vec_peers[at]))

    vec_step()
    if s.folds:
        mlp_folds[0].end_zl()
        mlp_folds[1].end_zl()
    end_x(0)
    vec_step()
    if s.folds:
        o_mlp[0] = mlp_folds[0].end_zh()
        o_mlp[1] = mlp_folds[1].end_zh()
    end_x(1)
    if s.folds:
        att_folds[0].end_y()
        vec_step()
    end_x(2)
    if s.folds:
        gathers = []

        def end_zh(t):
            v.ag[m, t] = att_folds[t].end_zh().astype(LOW)
            for peer in (peer_lo, peer_hi, peer_far):
                gathers.append(send(v.ag.at[m, t], v.ag.at[m, t], peer))

        att_folds[0].end_zl()
        att_folds[1].end_y()
        vec_step()
        att_folds[1].end_zl()
        end_zh(0)
        att_folds[2].end_y()
        vec_step()
        end_zh(1)
        att_folds[2].end_zl()
        end_zh(2)
        for copy in gathers:
            copy.wait_recv()
        o_att[...] = v.ag[...]
    vec_step()
    o_vec[...] = v.vec[len(vec_peers)]
    for copy in sent:
        copy.wait_send()


def spread_kernel(lengths, routed, tokens, cotangent, upd_out, upd_tok, mlp, att, vec, block_out, grad_tokens, g_up, g_down, g_qkv, g_out, g_vec):
    step = pl.program_id(0)
    rows, n = tokens.shape[1], routed.shape[1]
    block, d = g_out.shape
    wanted = jnp.where(iota((1, n), 1) < lengths[0] // 8, routed[...], -1)
    place = jnp.where(iota((rows, n), 0) + step * rows == wanted, 1.0, 0.0).astype(LOW)
    block_out[0] = (tokens[0].astype(F32) + mm(place, upd_out[...])).astype(LOW)
    grad_tokens[0] = (cotangent[0].astype(F32) + mm(place, upd_tok[...])).astype(LOW)

    @pl.when(step == 0)
    def _():
        g_up[...] = mlp[0]
        g_down[...] = mlp[1].T
        part = att.shape[3]
        for g in range(4):
            for t in range(att.shape[1]):
                piece = att[g, t].astype(F32)
                if g < 3:
                    g_qkv[:, g * d + t * part : g * d + (t + 1) * part] = piece
                else:
                    g_out[:, t * part : (t + 1) * part] = piece
        mine = iota((d, g_vec.shape[1]), 0) == iota((d, g_vec.shape[1]), 1) + lax.axis_index("batch") * block
        g_vec[...] = lax.dot_general(
            vec[...], jnp.where(mine, 1.0, 0.0), (((1,), (0,)), ((), ())),
            preferred_element_type=F32, precision=lax.Precision.HIGHEST,
        )


def local(tokens, key_mask, lengths, routed, w_router, gain_one, gain_two, w_qkv, w_out, w_up, w_down, cotangent):
    _, rows, d = tokens.shape
    n, f = routed.shape[1], w_up.shape[1]
    batch, mp = lax.axis_size("batch"), lax.axis_size("mp")
    s = Sizes(rows, d, n, f, batch)
    found = scratch_of(s)
    vmem, smem, anywhere = (pl.BlockSpec(memory_space=space) for space in (pltpu.VMEM, pltpu.SMEM, pl.ANY))
    if s.folds:
        mlp_shape, att_shape = jax.ShapeDtypeStruct((2, s.block, f), F32), jax.ShapeDtypeStruct((4, STAGES, s.block, s.part), LOW)
    else:
        mlp_shape, att_shape = jax.ShapeDtypeStruct((2, d, f), LOW), jax.ShapeDtypeStruct((STAGES, d, s.part), LOW)
    upd_out, upd_tok, mlp, att, vec = pl.pallas_call(
        functools.partial(layer_kernel, s, tuple(found)),
        out_shape=(
            jax.ShapeDtypeStruct((n, d), LOW),
            jax.ShapeDtypeStruct((n, d), LOW),
            mlp_shape,
            att_shape,
            jax.ShapeDtypeStruct((8, d), F32),
        ),
        in_specs=[anywhere, anywhere, vmem, smem, vmem, vmem, vmem, vmem, anywhere, anywhere, anywhere, anywhere],
        out_specs=[vmem] * 5,
        scratch_shapes=list(found.values()),
        compiler_params=pltpu.CompilerParams(collective_id=0, has_side_effects=True, vmem_limit_bytes=VMEM_BYTES),
        name="layer",
    )(
        tokens, cotangent, key_mask, lengths, routed,
        w_router.reshape(1, d), gain_one.reshape(1, d), gain_two.reshape(1, d),
        w_qkv, w_out, w_up, w_down,
    )
    if not s.folds:
        mlp = lax.psum_scatter(mlp.astype(F32), "batch", scatter_dimension=1, tiled=True)
        att = lax.psum_scatter(att.astype(F32), "batch", scatter_dimension=1, tiled=True).astype(LOW)
        att = lax.all_gather(att, "mp", axis=0)
        vec = lax.psum(vec, "batch")
    tile = rows // 4
    tiles = pl.BlockSpec((1, tile, d), lambda i: (0, i, 0))
    block_out, grad_tokens, g_up, g_down, g_qkv, g_out, g_vec = pl.pallas_call(
        spread_kernel,
        grid=(rows // tile,),
        out_shape=(
            jax.ShapeDtypeStruct(tokens.shape, LOW),
            jax.ShapeDtypeStruct(tokens.shape, LOW),
            jax.ShapeDtypeStruct((s.block, f), F32),
            jax.ShapeDtypeStruct((f, s.block), F32),
            jax.ShapeDtypeStruct((s.block, 3 * d), F32),
            jax.ShapeDtypeStruct((s.block, d), F32),
            jax.ShapeDtypeStruct((8, s.block), F32),
        ),
        in_specs=[smem, vmem, tiles, tiles, vmem, vmem, vmem, vmem, vmem],
        out_specs=[tiles, tiles, vmem, vmem, vmem, vmem, vmem],
        compiler_params=pltpu.CompilerParams(vmem_limit_bytes=VMEM_BYTES),
        name="spread",
    )(lengths, routed, tokens, cotangent, upd_out, upd_tok, mlp, att, vec)
    return block_out, grad_tokens, g_vec[0], g_vec[1], g_vec[2], g_qkv, g_out, g_up, g_down


def solution(mesh):
    rows_spec = P(("batch", "mp"), None, None)
    in_specs = (
        rows_spec,
        P(("batch", "mp"), None),
        P(("batch", "mp")),
        P(("batch", "mp"), None),
        P(),
        P(),
        P(),
        P(),
        P(),
        P(None, "mp"),
        P("mp", None),
        rows_spec,
    )
    out_specs = (
        rows_spec,
        rows_spec,
        P("batch"),
        P("batch"),
        P("batch"),
        P("batch", None),
        P("batch", None),
        P("batch", "mp"),
        P("mp", "batch"),
    )
    return jax.shard_map(local, mesh=mesh, in_specs=in_specs, out_specs=out_specs, check_vma=False)
```

```python
import functools
import itertools
import types

import jax
import jax.numpy as jnp
from jax import lax
from jax.experimental import pallas as pl
from jax.experimental.pallas import tpu as pltpu
from jax.sharding import PartitionSpec as P

HEADS = 12
EPSILON = 1e-06
LOW = jnp.bfloat16
F32 = jnp.float32
MESH = pl.DeviceIdType.MESH
VMEM_BYTES = 54 * 2**20
AXES = "dxbay"
MLP_ORDERS = ("ayb", "yab", "yab", "yab", "yab", "aby")
ATT_ORDERS = ("dxyab", "dxyab", "dxyab", "daxyb", "dyxab", "dxyab")
SEQUENCE = (
    ("f0", "f1", "u0", "u1", "u2", "u3", "u4", "u5", "w0", "w1", "w2", "w3", "w4", "w5", "r0", "r1", "b0", "m0", "m1"),
    ("b1", "a0", "b2", "a1", "m5", "m2", "b3", "a2", "m1", "b4", "a3", "m3", "b5", "a4", "a0", "m2", "m5", "e0", "a5"),
    ("m4", "m1", "e1", "a1", "m0", "a3", "v", "s0", "m3", "a4", "s1", "a2", "m2", "s2", "s3", "a0", "m4", "m5", "a5", "m0", "a1", "a0", "a3"),
    ("m3", "v", "a2", "a1", "m4", "a4", "a5", "a0", "a3", "a2", "v", "a1", "a4", "a0", "a5", "a0", "a1", "a3", "v"),
    ("a1", "a2", "a4", "a3", "a5", "a2", "a3", "v", "a4", "a2", "a5", "a4", "a5"),
)


def mm(a, b, along_a=1, along_b=0):
    return lax.dot_general(a, b, (((along_a,), (along_b,)), ((), ())), preferred_element_type=F32)


def norm_rate(v):
    return lax.rsqrt(jnp.mean(v * v, axis=1, keepdims=True) + EPSILON)


def gelu_and_slope(v):
    c = 0.7978845608028654
    square = v * v
    t = jnp.tanh(v * (c + (c * 0.044715) * square))
    half = 0.5 + 0.5 * t
    slope = half + (0.5 * v) * (1.0 - t * t) * (c + (c * 3 * 0.044715) * square)
    return v * half, slope


def iota(shape, dim):
    return lax.broadcasted_iota(jnp.int32, shape, dim)


class Sizes:
    def __init__(self, rows, width, slots, hidden, batch):
        self.rows, self.width, self.slots, self.hidden, self.batch = rows, width, slots, hidden, batch
        self.block = width // batch
        self.folds = batch == 8 and self.block % 16 == 0
        self.pair = 2 * (width // HEADS)
        self.pairs = HEADS // 2
        self.part = hidden // 3
        self.mlp_orders = MLP_ORDERS if self.folds else ("",) * len(MLP_ORDERS)
        self.att_orders = ATT_ORDERS if self.folds else ("dx",) * len(ATT_ORDERS)
        self.tail = (self.block,) if self.folds else (width,)

    def table(self, axes, columns):
        return (*(2 for axis in AXES if axis in axes), *self.tail, columns)


def scratch_of(s):
    n, d, f = s.slots, s.width, s.hidden
    found = dict(
        cot=pltpu.VMEM((s.rows, d), LOW),
        wqkv=pltpu.VMEM((d, 3 * d), LOW),
        wout=pltpu.VMEM((d, d), LOW),
        wup=pltpu.VMEM((2, d, f), LOW),
        wdn=pltpu.VMEM((2, f, d), LOW),
        pick=pltpu.VMEM((n, s.rows), LOW),
        picked=pltpu.VMEM((n, d), F32),
        cotr=pltpu.VMEM((n, d), LOW),
        first=pltpu.VMEM((n, d), LOW),
        qkv=pltpu.VMEM((n, 3 * d), LOW),
        bias=pltpu.VMEM((n, n), F32),
        probs=pltpu.VMEM((HEADS, n, n), LOW),
        mixed=pltpu.VMEM((n, d), LOW),
        first_t=pltpu.VMEM((d, n), LOW),
        mixed_t=pltpu.VMEM((d, n), LOW),
        sec_t=pltpu.VMEM((d, 2 * n), LOW),
        upd_out=pltpu.VMEM((n, d), LOW),
        upd_tok=pltpu.VMEM((n, d), LOW),
        gm_t=pltpu.VMEM((d, 2 * n), LOW),
        attended=pltpu.VMEM((n, d), F32),
        resid=pltpu.VMEM((n, d), F32),
        sec=pltpu.VMEM((2, n, d), LOW),
        gm=pltpu.VMEM((2, n, d), LOW),
        act=pltpu.VMEM((2, 2 * n, f), LOW),
        gpre=pltpu.VMEM((2, 2 * n, f), LOW),
        gs_own=pltpu.VMEM((n, d), F32),
        mo_own=pltpu.VMEM((n, d), F32),
        gs_out=pltpu.VMEM((n, d), LOW),
        mo_out=pltpu.VMEM((n, d), LOW),
        gs_in=pltpu.VMEM((n, d), LOW),
        mo_in=pltpu.VMEM((n, d), LOW),
        gres=pltpu.VMEM((n, d), F32),
        gatt=pltpu.VMEM((n, d), LOW),
        gmix=pltpu.VMEM((n, d), LOW),
        dqkv=pltpu.VMEM((n, 3 * d), LOW),
        vec=pltpu.VMEM((6, 8, d), F32),
        vec_in=pltpu.VMEM((5, 8, d), F32),
        send_sem=pltpu.SemaphoreType.DMA((112,)),
        recv_sem=pltpu.SemaphoreType.DMA((112,)),
        local_sem=pltpu.SemaphoreType.DMA((16,)),
    )
    batch_axes = "bay" if s.folds else ""
    for name, orders, axes, columns in (("m", s.mlp_orders, batch_axes, s.part), ("a", s.att_orders, "dx" + batch_axes, s.pair)):
        for at, order in enumerate(orders):
            left = axes
            found[f"{name}{at}_0"] = pltpu.VMEM(s.table(left, columns), LOW)
            for step, axis in enumerate(order):
                left = left.replace(axis, "")
                found[f"{name}{at}_{step + 1}"] = pltpu.VMEM(s.table(left, columns), LOW)
            if name == "m":
                found[f"u{at}"] = pltpu.VMEM(s.table(axes, columns), LOW)
    if s.folds:
        found["gathered"] = pltpu.VMEM((4, s.pairs, s.block, s.pair), LOW)
    return found


def layer_kernel(s, names, *refs):
    ins, outs, scratch = refs[:12], refs[12:21], refs[21:]
    tokens, cotangent, key_mask, lengths, routed, w_router, gain_one, gain_two, w_qkv, w_out, w_up, w_down = ins
    block_out, grad_tokens, o_up, o_down, o_qkv, o_out, *o_vecs = outs
    v = types.SimpleNamespace(**dict(zip(names, scratch, strict=True)), tok=block_out.at[0])
    n, d, f, pair = s.slots, s.width, s.hidden, s.pair
    half_rows = n // 2

    b, m = lax.axis_index("batch"), lax.axis_index("mp")
    lo, hi = m % 2, m // 2
    here = {"d": lo, "x": hi}
    peer = {"d": (b, m + 1 - 2 * lo), "x": (b, m + 2 - 4 * hi)}
    if s.folds:
        y, zl, zh = b % 2, (b // 2) % 2, b // 4
        here |= {"y": y, "a": zl, "b": zh}
        peer |= {"y": (b + 1 - 2 * y, m), "a": (b + 2 - 4 * zl, m), "b": (b + 4 - 8 * zh, m)}

    barrier = pltpu.get_barrier_semaphore()
    for other in peer.values():
        pl.semaphore_signal(barrier, inc=1, device_id=other, device_id_type=MESH)

    sent = []

    def send(src, dst, axis):
        at = len(sent)
        copy = pltpu.make_async_remote_copy(
            src_ref=src,
            dst_ref=dst,
            send_sem=v.send_sem.at[at],
            recv_sem=v.recv_sem.at[at],
            device_id=peer[axis],
            device_id_type=MESH,
        )
        copy.start()
        sent.append(copy)
        return copy

    fetches = []
    for src, dst in (
        (tokens.at[0], v.tok),
        (cotangent.at[0], v.cot),
        (w_qkv, v.wqkv),
        (w_out, v.wout),
        (w_up, v.wup.at[0]),
        (w_down, v.wdn.at[0]),
    ):
        fetches.append(pltpu.make_async_copy(src, dst, v.local_sem.at[len(fetches)]))
        fetches[-1].start()
    got_tok, got_cot, got_qkv, got_out, got_up, got_down = fetches

    live_count = lengths[0] // 8
    wanted = jnp.where(iota((1, n), 1) < live_count, routed[...], -1).astype(F32)
    on_diagonal = iota((n, n), 0) == iota((n, n), 1)
    wanted_column = jnp.sum(jnp.where(on_diagonal, wanted, 0.0), axis=1, keepdims=True).astype(jnp.int32)
    live = jnp.where(iota((n, 1), 0) < live_count, 1.0, 0.0)
    v.pick[...] = jnp.where(iota((n, s.rows), 1) == wanted_column, 1.0, 0.0).astype(LOW)

    got_tok.wait()
    picked = mm(v.pick[...], v.tok[...])
    v.picked[...] = picked
    router_row, one_row, two_row = (row[...].astype(F32).reshape(1, d) for row in (w_router, gain_one, gain_two))
    gate_rate = 1.0 / (1.0 + jnp.exp(-jnp.sum(picked * router_row, axis=1, keepdims=True)))
    route_gain = live * gate_rate

    got_cot.wait()
    cot_rows = mm(v.pick[...], v.cot[...])
    v.gm[0] = (route_gain * cot_rows).astype(LOW)

    pl.semaphore_wait(barrier, len(peer))
    sent_gm = send(v.gm.at[0], v.gm.at[1], "x")
    sent_up = send(w_up, v.wup.at[1], "d")
    sent_down = send(w_down, v.wdn.at[1], "d")

    v.cotr[...] = cot_rows.astype(LOW)
    rate_one = norm_rate(picked)
    v.first[...] = (picked * rate_one * one_row).astype(LOW)
    got_qkv.wait()
    for at in range(0, 3 * d, 256):
        v.qkv[:, at : at + 256] = mm(v.first[...], v.wqkv[:, at : at + 256]).astype(LOW)

    mask_rows = jnp.broadcast_to(key_mask[...].astype(F32), (8, s.rows)).astype(LOW)
    key_open = mm(mask_rows, v.pick[...], 1, 1)[0:1] > 0.5
    earlier = iota((n, n), 1) < iota((n, n), 0)
    v.bias[...] = jnp.where((earlier & key_open) | on_diagonal, 0.0, -1e30)

    lane = iota((n, pair), 1)
    side = [lane < pair // 2, lane >= pair // 2]

    def only(x, at):
        return jnp.where(side[at], x.astype(F32), 0.0).astype(LOW)

    for p in range(s.pairs):
        q, k, val = (v.qkv[:, g * d + p * pair : g * d + (p + 1) * pair] for g in range(3))
        q = (q.astype(F32) * (d // HEADS) ** -0.5).astype(LOW)
        total = 0.0
        for h in range(2):
            scores = mm(only(q, h), k, 1, 1) + v.bias[...]
            powers = jnp.exp(scores - jnp.max(scores, axis=1, keepdims=True))
            probs = (powers * (1.0 / jnp.sum(powers, axis=1, keepdims=True))).astype(LOW)
            v.probs[2 * p + h] = probs
            total = total + mm(probs, only(val, h))
        v.mixed[:, p * pair : (p + 1) * pair] = total.astype(LOW)

    got_out.wait()
    sent_sec = []
    for at in range(2):
        rows = slice(at * half_rows, (at + 1) * half_rows)
        there = pl.ds(at * half_rows, half_rows)
        attended = mm(v.mixed[rows], v.wout[...])
        v.attended[rows] = attended
        resid = v.picked[rows] + attended
        v.resid[rows] = resid
        v.sec[0, rows] = (resid * norm_rate(resid) * two_row).astype(LOW)
        sent_sec.append(send(v.sec.at[0, there], v.sec.at[1, there], "x"))

    got_up.wait()
    got_down.wait()

    def feed(j, start, count):
        x, g = v.sec[j, start : start + count], v.gm[j, start : start + count]
        gs, mo = 0.0, 0.0
        for w in range(2):
            rows = slice(j * n + start, j * n + start + count)
            act, slope = gelu_and_slope(mm(x, v.wup[w]))
            act = act.astype(LOW)
            v.act[w, rows] = act
            gpre = (mm(g, v.wdn[w], 1, 1) * slope).astype(LOW)
            v.gpre[w, rows] = gpre
            gs = gs + mm(gpre, v.wup[w], 1, 1)
            mo = mo + mm(act, v.wdn[w])
        return gs, mo

    sent_up.wait_recv()
    sent_down.wait_recv()
    v.gs_own[...], v.mo_own[...] = feed(0, 0, n)
    v.first_t[...] = v.first[...].T
    v.mixed_t[...] = v.mixed[...].T
    v.sec_t[:, :n] = v.sec[0].T
    v.gm_t[:, :n] = v.gm[0].T

    sent_gm.wait_recv()
    v.gm_t[:, n:] = v.gm[1].T
    sent_gs, sent_mo = [], []

    def feed_other(at):
        rows = slice(at * half_rows, (at + 1) * half_rows)
        there = pl.ds(at * half_rows, half_rows)
        sent_sec[at].wait_recv()
        gs, mo = feed(1, at * half_rows, half_rows)
        v.gs_out[rows] = gs.astype(LOW)
        sent_gs.append(send(v.gs_out.at[there], v.gs_in.at[there], "x"))
        v.mo_out[rows] = mo.astype(LOW)
        if at == 1:
            v.sec_t[:, n:] = v.sec[1].T
            for late in range(2):
                there = pl.ds(late * half_rows, half_rows)
                sent_mo.append(send(v.mo_out.at[there], v.mo_in.at[there], "x"))

    def weight_grad(at, w):
        left, right = (v.sec_t, v.gpre) if at < 3 else (v.gm_t, v.act)
        cols = slice(at % 3 * s.part, (at % 3 + 1) * s.part)
        return mm(left[...], right[w, :, cols])

    sent_core = []

    def other_core(at):
        table = getattr(v, f"u{at}")
        table[...] = weight_grad(at, 1).astype(LOW).reshape(table.shape)
        sent_core.append(send(table, getattr(v, f"m{at}_0"), "d"))

    class Sum:
        def __init__(self, name, axes, order, finish):
            self.name, self.axes, self.order, self.finish, self.at = name, axes, order, finish, 0
            if order:
                self.start()

        def table(self, at):
            return getattr(v, f"{self.name}_{at}")

        def start(self):
            axis = self.order[self.at]
            src = self.table(self.at).at[tuple(1 - here[k] if k == axis else slice(None) for k in self.axes)]
            self.going = send(src, self.table(self.at + 1), axis)

        def advance(self):
            if self.at == len(self.order):
                self.finish.advance()
                return
            axis = self.order[self.at]
            self.going.wait_recv()
            kept, arrived = self.table(self.at), self.table(self.at + 1)
            last = self.at + 1 == len(self.order)
            rest = self.axes.replace(axis, "")
            for index in itertools.product(*[range(2)] * len(rest)):
                full = dict(zip(rest, index, strict=True)) | {axis: here[axis]}
                total = arrived[index].astype(F32) + kept[tuple(full[k] for k in self.axes)].astype(F32)
                if last:
                    self.finish.begin(total)
                else:
                    arrived[index] = total.astype(LOW)
            self.axes, self.at = rest, self.at + 1
            if not last:
                self.start()

    class Store:
        def __init__(self, at):
            self.at = at

        def begin(self, total):
            out = o_up if self.at < 3 else o_down
            out[:, self.at % 3 * s.part : (self.at % 3 + 1) * s.part] = total

    class Gather:
        def __init__(self, p):
            self.p = p

        def begin(self, total):
            if not s.folds:
                o_qkv[self.p] = total
                return
            piece = v.gathered.at[m, self.p]
            piece[...] = total.astype(LOW)
            self.over_x = send(piece, piece, "x")
            self.over_d = send(piece, piece, "d")
            self.handed_on = None

        def advance(self):
            if self.handed_on is None:
                self.over_x.wait_recv()
                piece = v.gathered.at[m + 2 - 4 * hi, self.p]
                self.handed_on = send(piece, piece, "d")
            else:
                self.over_d.wait_recv()
                self.handed_on.wait_recv()
                for g in range(3):
                    o_qkv[:, g * d + self.p * pair : g * d + (self.p + 1) * pair] = v.gathered[g, self.p].astype(F32)
                o_out[:, self.p * pair : (self.p + 1) * pair] = v.gathered[3, self.p].astype(F32)

    sums = {}

    def own_core(at):
        own = weight_grad(at, 0)
        sent_core[at].wait_recv()
        table = getattr(v, f"m{at}_0")
        table[...] = (table[...].astype(F32) + own.reshape(table.shape)).astype(LOW)
        if s.folds:
            sums[f"m{at}"] = Sum(f"m{at}", "bay", s.mlp_orders[at], Store(at))
        else:
            out = o_up if at < 3 else o_down
            out[:, at % 3 * s.part : (at % 3 + 1) * s.part] = table[...].astype(F32)

    gain_two_sums = []

    def second_back(at):
        rows = slice(at * half_rows, (at + 1) * half_rows)
        sent_gs[at].wait_recv()
        gs = (v.gs_own[rows] + v.gs_in[rows].astype(F32)).astype(LOW).astype(F32)
        resid = v.resid[rows]
        rate = norm_rate(resid)
        gain_two_sums.append(jnp.sum(gs * (resid * rate), axis=0, keepdims=True))
        scaled = gs * two_row
        gres = rate * scaled - resid * (rate * rate * rate * jnp.mean(scaled * resid, axis=1, keepdims=True))
        v.gres[rows] = gres
        gatt = (route_gain[rows] * v.cotr[rows].astype(F32) + gres).astype(LOW)
        v.gatt[rows] = gatt
        v.gmix[rows] = mm(gatt, v.wout[...], 1, 1).astype(LOW)

    def attend_back(p):
        where = [slice(g * d + p * pair, g * d + (p + 1) * pair) for g in range(3)]
        q, k, val = (v.qkv[:, cols] for cols in where)
        gmix = v.gmix[:, p * pair : (p + 1) * pair]
        gq, gk, gv = 0.0, 0.0, 0.0
        for h in range(2):
            probs = v.probs[2 * p + h]
            gmix_h = only(gmix, h)
            gprobs = mm(gmix_h, val, 1, 1)
            wide = probs.astype(F32)
            product = gprobs * wide
            gscores = product - wide * jnp.sum(product, axis=1, keepdims=True)
            gscores = (gscores * (d // HEADS) ** -0.5).astype(LOW)
            gq = gq + mm(gscores, only(k, h))
            gk = gk + mm(gscores, only(q, h), 0, 0)
            gv = gv + mm(probs, gmix_h, 0, 0)
        table = getattr(v, f"a{p}_0")
        lower = []
        for cols, grad in zip(where, (gq, gk, gv), strict=True):
            lower.append(grad.astype(LOW))
            v.dqkv[:, cols] = lower[-1]
        both = mm(v.first_t[...], jnp.concatenate(lower[:2], axis=1)).astype(LOW)
        shape = table.shape[2:]
        table[0, 0] = both[:, :pair].reshape(shape)
        table[1, 0] = both[:, pair:].reshape(shape)
        table[0, 1] = mm(v.first_t[...], lower[2]).astype(LOW).reshape(shape)
        table[1, 1] = mm(v.mixed_t[...], v.gatt[:, p * pair : (p + 1) * pair]).astype(LOW).reshape(shape)
        sums[f"a{p}"] = Sum(f"a{p}", "dxbay" if s.folds else "dx", s.att_orders[p], Gather(p))

    kept = {}

    def first_back():
        gfirst = mm(v.dqkv[...], v.wqkv[...], 1, 1)
        picked = v.picked[...]
        kept["gain_one"] = jnp.sum(gfirst * (picked * rate_one), axis=0, keepdims=True)
        scaled = gfirst * one_row
        gnorm = rate_one * scaled - picked * (rate_one * rate_one * rate_one * jnp.mean(scaled * picked, axis=1, keepdims=True))
        v.gres[...] = v.gres[...] + gnorm

    def finish_rows():
        for copy in sent_mo:
            copy.wait_recv()
        picked = v.picked[...]
        branch = v.attended[...] + (v.mo_own[...] + v.mo_in[...].astype(F32)).astype(LOW).astype(F32)
        grate = live * jnp.sum(v.cotr[...].astype(F32) * branch, axis=1, keepdims=True)
        glogit = grate * gate_rate * (1.0 - gate_rate)
        router_sum = jnp.sum(glogit * picked, axis=0, keepdims=True)
        v.upd_out[...] = (route_gain * branch).astype(LOW)
        v.upd_tok[...] = (live * (v.gres[...] + glogit * router_row)).astype(LOW)
        row = iota((8, d), 0)
        gain_two_sum = gain_two_sums[0] + gain_two_sums[1]
        v.vec[0] = jnp.where(row == 0, router_sum, jnp.where(row == 1, kept["gain_one"], jnp.where(row == 2, gain_two_sum, 0.0)))
        sums["v"] = Everywhere("dxyab" if s.folds else "dx")

    tile = s.rows // 4
    writes = []

    def spread(at):
        rows = slice(at * tile, (at + 1) * tile)
        there = pl.ds(at * tile, tile)
        place = jnp.where(iota((tile, n), 0) + at * tile == wanted.astype(jnp.int32), 1.0, 0.0).astype(LOW)
        for table, update in ((v.tok, v.upd_out), (v.cot, v.upd_tok)):
            table[rows] = (table[rows].astype(F32) + mm(place, update[...])).astype(LOW)
        writes.append(pltpu.make_async_copy(v.cot.at[there], grad_tokens.at[0, there], v.local_sem.at[len(fetches) + at]))
        writes[-1].start()

    class Everywhere:
        def __init__(self, order):
            self.order, self.at = order, 0
            self.start()

        def start(self):
            self.going = send(v.vec.at[self.at], v.vec_in.at[self.at], self.order[self.at])

        def advance(self):
            self.going.wait_recv()
            v.vec[self.at + 1] = v.vec[self.at] + v.vec_in[self.at]
            self.at += 1
            if self.at < len(self.order):
                self.start()
            else:
                total = v.vec[self.at]
                if not s.folds:
                    for at, out in enumerate(o_vecs):
                        out[...] = total[at : at + 1]
                    return
                mine = iota((d, s.block), 0) == iota((d, s.block), 1) + b * s.block
                total = lax.dot_general(
                    total, jnp.where(mine, 1.0, 0.0), (((1,), (0,)), ((), ())),
                    preferred_element_type=F32, precision=lax.Precision.HIGHEST,
                )
                for at, out in enumerate(o_vecs):
                    out[...] = total[at : at + 1]

    work = {"f": feed_other, "u": other_core, "w": own_core, "r": second_back, "b": attend_back, "s": spread}
    for step in itertools.chain(*SEQUENCE):
        if step[0] in work:
            work[step[0]](int(step[1:]))
        elif step == "e0":
            first_back()
        elif step == "e1":
            finish_rows()
        elif s.folds:
            sums[step].advance()
    if not s.folds:
        for name, total in sums.items():
            total.advance()
            total.advance()
    for copy in sent:
        copy.wait_send()
    for copy in writes:
        copy.wait()


def hand_over_kernel(count, *refs):
    near, far, outs, held, sems = refs[0], refs[1:count], refs[count : 2 * count], refs[2 * count : -1], refs[-1]
    pieces = [(near, None, outs[0])]
    for src, dst, buf in zip(far, outs[1:], held, strict=True):
        cuts = 4 if src.shape[0] == 1 and src.ndim == 3 else 1
        if cuts == 1:
            pieces.append((src, buf, dst))
        else:
            rows = src.shape[1] // cuts
            pieces += [tuple(x.at[0, pl.ds(at * rows, rows)] for x in (src, buf, dst)) for at in range(cuts)]
    coming, going = {}, []
    for at, (src, buf, dst) in enumerate(pieces):
        if buf is not None:
            coming[at] = pltpu.make_async_copy(src, buf, sems.at[0, at])
            coming[at].start()
    for at, (src, buf, dst) in enumerate(pieces):
        if at in coming:
            coming[at].wait()
        going.append(pltpu.make_async_copy(src if buf is None else buf, dst, sems.at[1, at]))
        going[-1].start()
    for copy in going:
        copy.wait()


def hand_over(near, *far):
    arrays = (near, *far)
    anywhere = pl.BlockSpec(memory_space=pl.ANY)
    return pl.pallas_call(
        functools.partial(hand_over_kernel, len(arrays)),
        out_shape=[jax.ShapeDtypeStruct(x.shape, x.dtype) for x in arrays],
        in_specs=[pl.BlockSpec(memory_space=pltpu.VMEM)] + [pl.BlockSpec(memory_space=pltpu.HBM)] * len(far),
        out_specs=[anywhere] * len(arrays),
        scratch_shapes=[*[pltpu.VMEM(x.shape, x.dtype) for x in far], pltpu.SemaphoreType.DMA((2, len(arrays) + 3))],
        compiler_params=pltpu.CompilerParams(vmem_limit_bytes=16 * 2**20),
        name="hand_over",
    )(pltpu.with_memory_space_constraint(near, pltpu.VMEM), *(pltpu.with_memory_space_constraint(x, pltpu.HBM) for x in far))


def local(tokens, key_mask, lengths, routed, w_router, gain_one, gain_two, w_qkv, w_out, w_up, w_down, cotangent):
    _, rows, d = tokens.shape
    n, f = routed.shape[1], w_up.shape[1]
    batch = lax.axis_size("batch")
    s = Sizes(rows, d, n, f, batch)
    found = scratch_of(s)
    vmem, smem, anywhere = (pl.BlockSpec(memory_space=space) for space in (pltpu.VMEM, pltpu.SMEM, pl.ANY))
    def f32(*shape):
        return jax.ShapeDtypeStruct(shape, F32)

    piece = s.block if s.folds else d
    block_out, grad_tokens, g_up, g_down, g_qkv, g_out, *g_vecs = pl.pallas_call(
        functools.partial(layer_kernel, s, tuple(found)),
        out_shape=(
            pltpu.VMEM(tokens.shape, LOW),
            jax.ShapeDtypeStruct(tokens.shape, LOW),
            f32(piece, f),
            f32(piece, f),
            f32(piece, 3 * d) if s.folds else f32(s.pairs, d, s.pair),
            f32(piece, d),
            *[f32(1, piece)] * 3,
        ),
        in_specs=[anywhere, anywhere, vmem, smem, vmem, vmem, vmem, vmem, anywhere, anywhere, anywhere, anywhere],
        out_specs=[vmem, anywhere] + [vmem] * 7,
        scratch_shapes=list(found.values()),
        compiler_params=pltpu.CompilerParams(collective_id=0, has_side_effects=True, vmem_limit_bytes=VMEM_BYTES),
        name="layer",
    )(
        tokens, cotangent, key_mask, lengths, routed, w_router, gain_one, gain_two, w_qkv, w_out, w_up, w_down,
    )
    if not s.folds:
        g_up, g_down, *g_vecs = (lax.psum_scatter(g, "batch", scatter_dimension=g.ndim - 1 if g.shape[0] == 1 else 0, tiled=True) for g in (g_up, g_down, *g_vecs))
        att = lax.psum_scatter(g_qkv, "batch", scatter_dimension=1, tiled=True).astype(LOW)
        att = lax.all_gather(att, "mp", axis=0).astype(F32)
        att = jnp.transpose(att, (2, 0, 1, 3)).reshape(s.block, 4 * d)
        g_qkv, g_out = att[:, : 3 * d], att[:, 3 * d :]
    block_out, grad_tokens, g_up, g_down, g_qkv, g_out, *g_vecs = hand_over(
        block_out, grad_tokens, g_up, g_down, g_qkv, g_out, *g_vecs
    )
    g_router, g_one, g_two = (g.reshape(s.block) for g in g_vecs)
    return block_out, grad_tokens, g_router, g_one, g_two, g_qkv, g_out, g_up, g_down.T


def solution(mesh):
    rows_spec = P(("batch", "mp"), None, None)
    in_specs = (
        rows_spec,
        P(("batch", "mp"), None),
        P(("batch", "mp")),
        P(("batch", "mp"), None),
        P(),
        P(),
        P(),
        P(),
        P(),
        P(None, "mp"),
        P("mp", None),
        rows_spec,
    )
    out_specs = (
        rows_spec,
        rows_spec,
        P("batch"),
        P("batch"),
        P("batch"),
        P("batch", None),
        P("batch", None),
        P("batch", "mp"),
        P("mp", "batch"),
    )
    return jax.shard_map(local, mesh=mesh, in_specs=in_specs, out_specs=out_specs, check_vma=False)
```

```python
import functools
import itertools
import types

import jax
import jax.numpy as jnp
from jax import lax
from jax.experimental import pallas as pl
from jax.experimental.pallas import tpu as pltpu
from jax.sharding import PartitionSpec as P

HEADS = 12
EPSILON = 1e-06
LOW = jnp.bfloat16
F32 = jnp.float32
MESH = pl.DeviceIdType.MESH
VMEM_BYTES = 58 * 2**20
AXES = "dxbay"
MLP_ORDERS = ("yab", "aby", "yab", "yab", "aby", "yab")
ATT_ORDERS = ("dxyab", "dxyab", "dxaby", "dyxabG", "dxyabG", "daxyb")
SEQUENCE = (
    ("f0", "f1", "u0", "u1", "u2", "u3", "u4", "u5", "w0", "w1", "w2", "w3", "w4", "t", "r0", "r1", "w5"),
    ("r2", "r3", "b0", "m1", "b1", "m0", "a0", "b2", "a1", "b3", "m4", "a2", "m2", "b4", "a3", "o0", "b5"),
    ("a4", "m0", "e0", "m1", "a5", "a0", "m3", "e1", "m2", "m4", "m5", "a1", "m0", "a3", "a5", "a2", "o1"),
    ("m3", "z", "m1", "s0", "s1", "a4", "v", "m2", "a0", "m5", "s2", "s3", "m4", "a3", "s4", "s5", "a2", "s6"),
    ("s7", "a5", "a1", "v", "a0", "m3", "a4", "a3", "m5", "a5", "v", "a1", "a2", "a4", "a0", "a3", "v", "a5"),
    ("a2", "a1", "a0", "a4", "a0", "a3", "a5", "a2", "v", "a1", "a5", "a2", "a1", "a4"),
)


def mm(a, b, along_a=1, along_b=0):
    return lax.dot_general(a, b, (((along_a,), (along_b,)), ((), ())), preferred_element_type=F32)


def norm_rate(v):
    return lax.rsqrt(jnp.mean(v * v, axis=1, keepdims=True) + EPSILON)


def gelu_and_slope(v):
    c = 0.7978845608028654
    square = v * v
    t = jnp.tanh(v * (c + (c * 0.044715) * square))
    half = 0.5 + 0.5 * t
    slope = half + (0.5 * v) * (1.0 - t * t) * (c + (c * 3 * 0.044715) * square)
    return v * half, slope


def iota(shape, dim):
    return lax.broadcasted_iota(jnp.int32, shape, dim)


class Sizes:
    def __init__(self, rows, width, slots, hidden, batch):
        self.rows, self.width, self.slots, self.hidden, self.batch = rows, width, slots, hidden, batch
        self.block = width // batch
        self.folds = batch == 8 and self.block % 16 == 0
        self.pair = 2 * (width // HEADS)
        self.pairs = HEADS // 2
        self.part = hidden // 3
        self.half, self.work = slots // 2, slots * 3 // 4
        self.spill = slots - self.work
        self.mlp_orders = MLP_ORDERS if self.folds else ("",) * len(MLP_ORDERS)
        self.att_orders = ATT_ORDERS if self.folds else ("dx",) * len(ATT_ORDERS)
        self.tail = (self.block,) if self.folds else (width,)

    def table(self, axes, columns):
        return (*(2 for axis in AXES if axis in axes), *self.tail, columns)


def scratch_of(s):
    n, d, f = s.slots, s.width, s.hidden
    found = dict(
        cot=pltpu.VMEM((s.rows, d), LOW),
        wqkv=pltpu.VMEM((d, 3 * d), LOW),
        wout=pltpu.VMEM((d, d), LOW),
        wup=pltpu.VMEM((2, d, f), LOW),
        wdn=pltpu.VMEM((2, f, d), LOW),
        wout_t=pltpu.VMEM((d, d), LOW),
        wup_t=pltpu.VMEM((2, f, d), LOW),
        wdn_t=pltpu.VMEM((2, d, f), LOW),
        pick=pltpu.VMEM((n, s.rows), LOW),
        picked=pltpu.VMEM((n, d), F32),
        cotr=pltpu.VMEM((n, d), LOW),
        first=pltpu.VMEM((n, d), LOW),
        qkv=pltpu.VMEM((n, 3 * d), LOW),
        bias=pltpu.VMEM((n, n), F32),
        probs=pltpu.VMEM((HEADS, n, n), LOW),
        mixed=pltpu.VMEM((n, d), LOW),
        first_t=pltpu.VMEM((d, n), LOW),
        mixed_t=pltpu.VMEM((d, n), LOW),
        sec_t=pltpu.VMEM((d, 2 * s.work), LOW),
        gm_t=pltpu.VMEM((d, 2 * s.work), LOW),
        upd_out=pltpu.VMEM((n, d), LOW),
        upd_tok=pltpu.VMEM((n, d), LOW),
        attended=pltpu.VMEM((n, d), F32),
        resid=pltpu.VMEM((n, d), F32),
        sec=pltpu.VMEM((2 * s.work, d), LOW),
        gm=pltpu.VMEM((2 * s.work, d), LOW),
        act=pltpu.VMEM((2, 2 * s.work, f), LOW),
        gpre=pltpu.VMEM((2, 2 * s.work, f), LOW),
        gs_own=pltpu.VMEM((s.work, d), F32),
        mo_own=pltpu.VMEM((s.work, d), F32),
        gs_out=pltpu.VMEM((s.work, d), LOW),
        mo_out=pltpu.VMEM((s.work, d), LOW),
        gs_in=pltpu.VMEM((s.work, d), LOW),
        mo_in=pltpu.VMEM((s.work, d), LOW),
        spill_out=pltpu.VMEM((4, s.spill, d), LOW),
        spill_in=pltpu.VMEM((5, s.spill, d), LOW),
        mo=pltpu.VMEM((n, d), F32),
        mask_row=pltpu.VMEM((1, s.rows), jnp.int32),
        wanted_row=pltpu.VMEM((1, n), jnp.int32),
        gres=pltpu.VMEM((n, d), F32),
        gatt=pltpu.VMEM((n, d), LOW),
        gmix=pltpu.VMEM((n, d), LOW),
        dqkv=pltpu.VMEM((n, 3 * d), LOW),
        vec=pltpu.VMEM((6, 8, d), F32),
        vec_in=pltpu.VMEM((5, 8, d), F32),
        send_sem=pltpu.SemaphoreType.DMA((112,)),
        recv_sem=pltpu.SemaphoreType.DMA((112,)),
        summed=pltpu.VMEM((2, *s.tail, f), F32),
        router=pltpu.VMEM((d,), LOW),
        one=pltpu.VMEM((d,), LOW),
        two=pltpu.VMEM((d,), LOW),
        write_sem=pltpu.SemaphoreType.DMA((12,)),
        local_sem=pltpu.SemaphoreType.DMA((24,)),
    )
    batch_axes = "bay" if s.folds else ""
    for name, orders, axes, columns in (("m", s.mlp_orders, batch_axes, s.part), ("a", s.att_orders, "dx" + batch_axes, s.pair)):
        for at, order in enumerate(orders):
            left = axes
            found[f"{name}{at}_0"] = pltpu.VMEM(s.table(left, columns), LOW)
            for step, axis in enumerate(order.strip("G")):
                left = left.replace(axis, "")
                found[f"{name}{at}_{step + 1}"] = pltpu.VMEM(s.table(left, columns), LOW)
            if name == "m":
                found[f"u{at}"] = pltpu.VMEM(s.table(axes, columns), LOW)
    if s.folds:
        found["gathered"] = pltpu.VMEM((4, s.pairs, s.block, s.pair), LOW)
    return found


def layer_kernel(s, names, *refs):
    ins, outs, scratch = refs[:12], refs[12:17], refs[17:]
    tokens, cotangent, key_mask, lengths, routed, w_router, gain_one, gain_two, w_qkv, w_out, w_up, w_down = ins
    block_out, o_att, o_vec, grad_tokens, o_mlp = outs
    v = types.SimpleNamespace(**dict(zip(names, scratch, strict=True)), tok=block_out.at[0])
    n, d, f, pair = s.slots, s.width, s.hidden, s.pair
    half_rows = n // 2

    b, m = lax.axis_index("batch"), lax.axis_index("mp")
    lo, hi = m % 2, m // 2
    y = b % 2
    here = {"d": lo, "x": hi, "y": y}
    other_m = {"d": m + 1 - 2 * lo, "x": m + 2 - 4 * hi, "f": 3 - m}
    peer = {axis: (b, to) for axis, to in other_m.items()} | {"y": (b + 1 - 2 * y, m), "q": (b + 1 - 2 * y, other_m["x"])}
    if s.folds:
        zl, zh = (b // 2) % 2, b // 4
        here |= {"a": zl, "b": zh}
        peer |= {"a": (b + 2 - 4 * zl, m), "b": (b + 4 - 8 * zh, m)}

    barrier = pltpu.get_barrier_semaphore()
    for other in peer.values():
        pl.semaphore_signal(barrier, inc=1, device_id=other, device_id_type=MESH)

    sent = []

    def send(src, dst, axis):
        at = len(sent)
        copy = pltpu.make_async_remote_copy(
            src_ref=src,
            dst_ref=dst,
            send_sem=v.send_sem.at[at],
            recv_sem=v.recv_sem.at[at],
            device_id=peer[axis],
            device_id_type=MESH,
        )
        copy.start()
        sent.append(copy)
        return copy

    fetches = []

    def fetch(src, dst):
        fetches.append(pltpu.make_async_copy(src, dst, v.local_sem.at[len(fetches)]))
        fetches[-1].start()
        return fetches[-1]

    writes, stored = [], []

    def write(src, dst):
        writes.append(pltpu.make_async_copy(src, dst, v.write_sem.at[len(writes)]))
        writes[-1].start()

    quarter = s.rows // 4
    quarters = [pl.ds(at * quarter, quarter) for at in range(4)]
    got_wanted = fetch(routed, v.wanted_row)
    got_rows = [fetch(src, dst) for src, dst in ((w_router, v.router), (gain_one, v.one), (gain_two, v.two))]
    got_tok = [fetch(tokens.at[0, there], v.tok.at[there]) for there in quarters]
    got_cot = [fetch(cotangent.at[0, there], v.cot.at[there]) for there in quarters]
    got_mask = fetch(key_mask, v.mask_row)

    got_wanted.wait()
    live_count = lengths[0] // 8
    wanted = jnp.where(iota((1, n), 1) < live_count, v.wanted_row[...], -1).astype(F32)
    on_diagonal = iota((n, n), 0) == iota((n, n), 1)
    wanted_column = jnp.sum(jnp.where(on_diagonal, wanted, 0.0), axis=1, keepdims=True).astype(jnp.int32)
    live = jnp.where(iota((n, 1), 0) < live_count, 1.0, 0.0)
    v.pick[...] = jnp.where(iota((n, s.rows), 1) == wanted_column, 1.0, 0.0).astype(LOW)

    def gather(table, got):
        total = 0.0
        for at in range(4):
            got[at].wait()
            cols = slice(at * quarter, (at + 1) * quarter)
            total = total + mm(v.pick[:, cols], table[cols])
        return total

    picked = gather(v.tok, got_tok)
    v.picked[...] = picked
    for got in got_rows:
        got.wait()
    router_row, one_row, two_row = (row[...].astype(F32).reshape(1, d) for row in (v.router, v.one, v.two))
    gate_rate = 1.0 / (1.0 + jnp.exp(-jnp.sum(picked * router_row, axis=1, keepdims=True)))
    route_gain = live * gate_rate

    got_qkv = fetch(w_qkv, v.wqkv)
    cot_rows = gather(v.cot, got_cot)
    got_out = fetch(w_out, v.wout)
    got_up = fetch(w_up, v.wup.at[0])
    got_down = fetch(w_down, v.wdn.at[0])
    half, work, spill = s.half, s.work, s.spill
    mine_a, other_a = pl.ds(0, half), pl.ds(half, half)
    mine_b, other_b = pl.ds(2 * half, spill), pl.ds(2 * half + spill, spill)
    gm = (route_gain * cot_rows).astype(LOW)
    v.gm[0:half] = gm[:half]
    v.spill_out[0] = gm[work:]

    pl.semaphore_wait(barrier, len(peer))
    sent_gm = [send(v.gm.at[mine_a], v.gm.at[other_a], "x")]
    spilt_gm = send(v.spill_out.at[0], v.spill_in.at[0], "y")
    sent_up = send(w_up, v.wup.at[1], "d")
    sent_down = send(w_down, v.wdn.at[1], "d")

    v.cotr[...] = cot_rows.astype(LOW)
    rate_one = norm_rate(picked)
    v.first[...] = (picked * rate_one * one_row).astype(LOW)
    got_qkv.wait()
    for at in range(0, 3 * d, 256):
        v.qkv[:, at : at + 256] = mm(v.first[...], v.wqkv[:, at : at + 256]).astype(LOW)

    place_spill = jnp.where(iota((spill, spill), 0) + half - live_count == iota((spill, spill), 1), 1.0, 0.0).astype(LOW)
    live_b = live[half:work]

    def merge(own, arrived):
        return (own.astype(F32) * live_b + mm(place_spill, arrived)).astype(LOW)

    def part_back(merged):
        return mm(place_spill, merged, 0, 0).astype(LOW)

    peer_live = 2 * work - live_count
    place_peer = jnp.where(iota((spill, spill), 0) + half - peer_live == iota((spill, spill), 1), 1.0, 0.0).astype(LOW)

    spilt_gm.wait_recv()
    v.gm[2 * half : 2 * half + spill] = merge(gm[half:work], v.spill_in[0])
    sent_gm.append(send(v.gm.at[mine_b], v.gm.at[other_b], "x"))

    got_mask.wait()
    mask_rows = jnp.broadcast_to(v.mask_row[...].astype(F32), (8, s.rows)).astype(LOW)
    key_open = mm(mask_rows, v.pick[...], 1, 1)[0:1] > 0.5
    earlier = iota((n, n), 1) < iota((n, n), 0)
    v.bias[...] = jnp.where((earlier & key_open) | on_diagonal, 0.0, -1e30)

    lane = iota((n, pair), 1)
    side = [lane < pair // 2, lane >= pair // 2]

    def only(x, at):
        return jnp.where(side[at], x.astype(F32), 0.0).astype(LOW)

    for p in range(s.pairs):
        q, k, val = (v.qkv[:, g * d + p * pair : g * d + (p + 1) * pair] for g in range(3))
        q = (q.astype(F32) * (d // HEADS) ** -0.5).astype(LOW)
        total = 0.0
        for h in range(2):
            scores = mm(only(q, h), k, 1, 1) + v.bias[...]
            powers = jnp.exp(scores - jnp.max(scores, axis=1, keepdims=True))
            probs = (powers * (1.0 / jnp.sum(powers, axis=1, keepdims=True))).astype(LOW)
            v.probs[2 * p + h] = probs
            total = total + mm(probs, only(val, h))
        v.mixed[:, p * pair : (p + 1) * pair] = total.astype(LOW)

    got_out.wait()

    def second(start, stop):
        rows = slice(start, stop)
        attended = mm(v.mixed[rows], v.wout[...])
        v.attended[rows] = attended
        resid = v.picked[rows] + attended
        v.resid[rows] = resid
        return (resid * norm_rate(resid) * two_row).astype(LOW)

    normed = second(0, n)
    v.spill_out[1] = normed[work:]
    spilt_sec = send(v.spill_out.at[1], v.spill_in.at[1], "y")
    v.sec[0:half] = normed[:half]
    sent_sec = [send(v.sec.at[mine_a], v.sec.at[other_a], "x")]
    second_b = normed[half:work]

    def feed(start, count):
        rows = slice(start, start + count)
        x, g = v.sec[rows], v.gm[rows]
        gs = 0.0
        for w in range(2):
            act, slope = gelu_and_slope(mm(x, v.wup[w]))
            v.act[w, rows] = act.astype(LOW)
            gpre = (mm(g, v.wdn_t[w]) * slope).astype(LOW)
            v.gpre[w, rows] = gpre
            gs = gs + mm(gpre, v.wup_t[w])
        return gs

    def feed_out(start, count):
        rows = slice(start, start + count)
        return mm(v.act[0, rows], v.wdn[0]) + mm(v.act[1, rows], v.wdn[1])

    got_up.wait()
    got_down.wait()
    sent_up.wait_recv()
    sent_down.wait_recv()
    for w in range(2):
        v.wup_t[w] = v.wup[w].T
        v.wdn_t[w] = v.wdn[w].T
    v.gs_own[0:half] = feed(0, half)
    spilt_sec.wait_recv()
    v.sec[2 * half : 2 * half + spill] = merge(second_b, v.spill_in[1])
    sent_sec.append(send(v.sec.at[mine_b], v.sec.at[other_b], "x"))
    gs = feed(2 * half, spill)
    v.gs_own[half:work] = gs
    v.spill_out[2] = gs.astype(LOW)
    spilt_own = send(v.spill_out.at[2], v.spill_in.at[2], "y")
    v.mo_own[0:half] = feed_out(0, half)
    v.mo_own[half:work] = feed_out(2 * half, spill)
    v.sec_t[:, :half] = v.sec[0:half].T
    v.gm_t[:, :half] = v.gm[0:half].T
    for copy in sent_gm:
        copy.wait_recv()
    v.gm_t[:, half:] = v.gm[half:].T
    sent_gs, sent_mo, spilt = [], [], {}

    def transposes():
        v.wout_t[...] = v.wout[...].T
        v.first_t[...] = v.first[...].T
        v.mixed_t[...] = v.mixed[...].T

    def send_back(out, into, start, count):
        there = pl.ds(start, count)
        return send(out.at[there], into.at[there], "x")

    def feed_other(at):
        sent_sec[at].wait_recv()
        start, count, into = (half, half, 0) if at == 0 else (2 * half + spill, spill, half)
        rows = slice(into, into + count)
        v.gs_out[rows] = feed(start, count).astype(LOW)
        if at == 0:
            sent_gs.append(send_back(v.gs_out, v.gs_in, 0, half // 2))
        else:
            sent_gs.append(send_back(v.gs_out, v.gs_in, half, spill))
            spilt["gs"] = send(v.gs_out.at[pl.ds(half, spill)], v.spill_in.at[4], "q")
            sent_gs.append(send_back(v.gs_out, v.gs_in, half // 2, half // 2))
        v.mo_out[rows] = feed_out(start, count).astype(LOW)
        if at == 1:
            sent_mo.append(send_back(v.mo_out, v.mo_in, half, spill))
            sent_mo.append(send_back(v.mo_out, v.mo_in, 0, half))
            v.sec_t[:, half:] = v.sec[half:].T

    def weight_grad(at, w):
        left, right = (v.sec_t, v.gpre) if at < 3 else (v.gm_t, v.act)
        cols = slice(at % 3 * s.part, (at % 3 + 1) * s.part)
        return mm(left[...], right[w, :, cols])

    sent_core = []

    def other_core(at):
        table = getattr(v, f"u{at}")
        table[...] = weight_grad(at, 1).astype(LOW).reshape(table.shape)
        sent_core.append(send(table, getattr(v, f"m{at}_0"), "d"))

    class Sum:
        def __init__(self, name, axes, order, finish):
            self.name, self.axes, self.order, self.finish, self.at = name, axes, order, finish, 0
            if order:
                self.start()

        def table(self, at):
            return getattr(v, f"{self.name}_{at}")

        def start(self):
            axis = self.order[self.at]
            src = self.table(self.at).at[tuple(1 - here[k] if k == axis else slice(None) for k in self.axes)]
            self.going = send(src, self.table(self.at + 1), axis)

        def advance(self):
            if self.at == len(self.order):
                self.finish.advance()
                return
            axis = self.order[self.at]
            self.going.wait_recv()
            kept, arrived = self.table(self.at), self.table(self.at + 1)
            last = self.at + 1 == len(self.order)
            rest = self.axes.replace(axis, "")
            for index in itertools.product(*[range(2)] * len(rest)):
                full = dict(zip(rest, index, strict=True)) | {axis: here[axis]}
                total = arrived[index].astype(F32) + kept[tuple(full[k] for k in self.axes)].astype(F32)
                if last:
                    self.finish.begin(total)
                else:
                    arrived[index] = total.astype(LOW)
            self.axes, self.at = rest, self.at + 1
            if not last:
                self.start()

    class Store:
        def __init__(self, at):
            self.at = at

        def begin(self, total):
            kind, cols = self.at // 3, slice(self.at % 3 * s.part, (self.at % 3 + 1) * s.part)
            v.summed[kind, :, cols] = total
            stored.append(self.at)
            if all(3 * kind + at in stored for at in range(3)):
                write(v.summed.at[kind], o_mlp.at[kind])

    class Gather:
        def __init__(self, p, direct):
            self.p, self.direct = p, direct

        def begin(self, total):
            if not s.folds:
                o_att[self.p] = total
                return
            piece = v.gathered.at[m, self.p]
            piece[...] = total.astype(LOW)
            self.over_x = send(piece, piece, "x")
            self.others = [send(piece, piece, "d")]
            if self.direct:
                self.others.append(send(piece, piece, "f"))
            self.handed_on = self.direct

        def advance(self):
            if not self.handed_on:
                self.over_x.wait_recv()
                piece = v.gathered.at[other_m["x"], self.p]
                self.others.append(send(piece, piece, "d"))
                self.handed_on = True
                return
            if self.direct:
                self.over_x.wait_recv()
            for copy in self.others:
                copy.wait_recv()
            for g in range(4):
                o_att[g, self.p] = v.gathered[g, self.p]

    sums = {}

    def own_core(at):
        own = weight_grad(at, 0)
        sent_core[at].wait_recv()
        table = getattr(v, f"m{at}_0")
        table[...] = (table[...].astype(F32) + own.reshape(table.shape)).astype(LOW)
        if s.folds:
            sums[f"m{at}"] = Sum(f"m{at}", "bay", s.mlp_orders[at], Store(at))
        else:
            v.summed[at // 3, :, at % 3 * s.part : (at % 3 + 1) * s.part] = table[...].astype(F32)
            if at % 3 == 2:
                write(v.summed.at[at // 3], o_mlp.at[at // 3])

    gain_two_sums = []

    def second_back(at):
        if at < 3:
            start, stop = ((0, half // 2), (half, work), (half // 2, half))[at]
            sent_gs[at].wait_recv()
            gs = (v.gs_own[start:stop] + v.gs_in[start:stop].astype(F32)).astype(LOW)
            if at == 1:
                gs = gs.astype(F32) * live_b
        else:
            start, stop = work, n
            spilt_own.wait_recv()
            spilt["gs"].wait_recv()
            gs = mm(place_peer, (v.spill_in[2].astype(F32) + v.spill_in[4].astype(F32)).astype(LOW), 0, 0)
        rows = slice(start, stop)
        gs = gs.astype(F32)
        resid = v.resid[rows]
        rate = norm_rate(resid)
        gain_two_sums.append(jnp.sum(gs * (resid * rate), axis=0, keepdims=True))
        scaled = gs * two_row
        gres = rate * scaled - resid * (rate * rate * rate * jnp.mean(scaled * resid, axis=1, keepdims=True))
        v.gres[rows] = gres
        gatt = (route_gain[rows] * v.cotr[rows].astype(F32) + gres).astype(LOW)
        v.gatt[rows] = gatt
        v.gmix[rows] = mm(gatt, v.wout_t[...]).astype(LOW)

    def part_mo(at):
        if at == 0:
            sent_mo[0].wait_recv()
            mo = (v.mo_own[half:work] + v.mo_in[half:work].astype(F32)).astype(LOW)
            v.spill_out[3] = part_back(mo)
            spilt["mo"] = send(v.spill_out.at[3], v.spill_in.at[3], "y")
            v.mo[half:work] = mo.astype(F32)
        else:
            sent_mo[1].wait_recv()
            v.mo[0:half] = (v.mo_own[0:half] + v.mo_in[0:half].astype(F32)).astype(LOW).astype(F32)
            spilt["mo"].wait_recv()
            v.mo[work:n] = v.spill_in[3].astype(F32)

    def attend_back(p):
        where = [slice(g * d + p * pair, g * d + (p + 1) * pair) for g in range(3)]
        q, k, val = (v.qkv[:, cols] for cols in where)
        gmix = v.gmix[:, p * pair : (p + 1) * pair]
        gq, gk, gv = 0.0, 0.0, 0.0
        for h in range(2):
            probs = v.probs[2 * p + h]
            gmix_h = only(gmix, h)
            gprobs = mm(gmix_h, val, 1, 1)
            wide = probs.astype(F32)
            product = gprobs * wide
            gscores = product - wide * jnp.sum(product, axis=1, keepdims=True)
            gscores = (gscores * (d // HEADS) ** -0.5).astype(LOW)
            gq = gq + mm(gscores, only(k, h))
            gk = gk + mm(gscores, only(q, h), 0, 0)
            gv = gv + mm(probs, gmix_h, 0, 0)
        table = getattr(v, f"a{p}_0")
        lower = []
        for cols, grad in zip(where, (gq, gk, gv), strict=True):
            lower.append(grad.astype(LOW))
            v.dqkv[:, cols] = lower[-1]
        both = mm(v.first_t[...], jnp.concatenate(lower[:2], axis=1)).astype(LOW)
        shape = table.shape[2:]
        table[0, 0] = both[:, :pair].reshape(shape)
        table[1, 0] = both[:, pair:].reshape(shape)
        table[0, 1] = mm(v.first_t[...], lower[2]).astype(LOW).reshape(shape)
        table[1, 1] = mm(v.mixed_t[...], v.gatt[:, p * pair : (p + 1) * pair]).astype(LOW).reshape(shape)
        order = s.att_orders[p]
        sums[f"a{p}"] = Sum(f"a{p}", "dxbay" if s.folds else "dx", order.strip("G"), Gather(p, "G" in order))

    kept = {}

    def first_back(at):
        rows = slice(at * half, (at + 1) * half)
        gfirst = mm(v.dqkv[rows], v.wqkv[...], 1, 1)
        picked, rate = v.picked[rows], rate_one[rows]
        kept[at] = jnp.sum(gfirst * (picked * rate), axis=0, keepdims=True)
        scaled = gfirst * one_row
        gnorm = rate * scaled - picked * (rate * rate * rate * jnp.mean(scaled * picked, axis=1, keepdims=True))
        v.gres[rows] = v.gres[rows] + gnorm

    def finish_rows():
        picked = v.picked[...]
        branch = v.attended[...] + v.mo[...]
        grate = live * jnp.sum(v.cotr[...].astype(F32) * branch, axis=1, keepdims=True)
        glogit = grate * gate_rate * (1.0 - gate_rate)
        router_sum = jnp.sum(glogit * picked, axis=0, keepdims=True)
        v.upd_out[...] = (route_gain * branch).astype(LOW)
        v.upd_tok[...] = (live * (v.gres[...] + glogit * router_row)).astype(LOW)
        row = iota((8, d), 0)
        gain_two_sum = sum(gain_two_sums)
        v.vec[0] = jnp.where(row == 0, router_sum, jnp.where(row == 1, kept[0] + kept[1], jnp.where(row == 2, gain_two_sum, 0.0)))
        sums["v"] = Everywhere("dxyab" if s.folds else "dx")

    tile = s.rows // 8

    def spread(at):
        rows = slice(at * tile, (at + 1) * tile)
        there = pl.ds(at * tile, tile)
        place = jnp.where(iota((tile, n), 0) + at * tile == wanted.astype(jnp.int32), 1.0, 0.0).astype(LOW)
        for table, update in ((v.tok, v.upd_out), (v.cot, v.upd_tok)):
            table[rows] = (table[rows].astype(F32) + mm(place, update[...])).astype(LOW)
        write(v.cot.at[there], grad_tokens.at[0, there])

    class Everywhere:
        def __init__(self, order):
            self.order, self.at = order, 0
            self.start()

        def start(self):
            self.going = send(v.vec.at[self.at], v.vec_in.at[self.at], self.order[self.at])

        def advance(self):
            self.going.wait_recv()
            v.vec[self.at + 1] = v.vec[self.at] + v.vec_in[self.at]
            self.at += 1
            if self.at < len(self.order):
                self.start()
            else:
                total = v.vec[self.at]
                if not s.folds:
                    o_vec[...] = total
                    return
                mine = iota((d, s.block), 0) == iota((d, s.block), 1) + b * s.block
                o_vec[...] = lax.dot_general(
                    total, jnp.where(mine, 1.0, 0.0), (((1,), (0,)), ((), ())),
                    preferred_element_type=F32, precision=lax.Precision.HIGHEST,
                )

    steps = {"f": feed_other, "u": other_core, "w": own_core, "r": second_back, "b": attend_back, "s": spread, "o": part_mo, "e": first_back}
    for step in itertools.chain(*SEQUENCE):
        if step[0] in steps:
            steps[step[0]](int(step[1:]))
        elif step == "t":
            transposes()
        elif step == "z":
            finish_rows()
        elif s.folds:
            sums[step].advance()
    if not s.folds:
        for name, total in sums.items():
            total.advance()
            total.advance()
    for copy in sent:
        copy.wait_send()
    for copy in writes:
        copy.wait()


def hand_over_kernel(block_out, att, vec, grad_tokens, mlp, out, tok, g_up, g_down, g_qkv, g_out, *rest):
    *vecs, tok_buf, mlp_buf, qkv_buf, out_buf, come_sem, go_sem = rest
    _, pairs, _, pair = att.shape
    d = g_out.shape[1]
    rows = tok.shape[1] // 4
    going = []

    def go(src, dst):
        going.append(pltpu.make_async_copy(src, dst, go_sem.at[len(going)]))
        going[-1].start()

    coming = []
    for src, dst in (
        *[(grad_tokens.at[0, pl.ds(at * rows, rows)], tok_buf.at[pl.ds(at * rows, rows)]) for at in range(4)],
        *[(mlp.at[at], mlp_buf.at[at]) for at in range(2)],
    ):
        coming.append(pltpu.make_async_copy(src, dst, come_sem.at[len(coming)]))
        coming[-1].start()
    go(block_out, out)
    for p in range(pairs):
        for g in range(3):
            qkv_buf[:, g * d + p * pair : g * d + (p + 1) * pair] = att[g, p].astype(F32)
        out_buf[:, p * pair : (p + 1) * pair] = att[3, p].astype(F32)
    go(qkv_buf, g_qkv)
    go(out_buf, g_out)
    for at, row in enumerate(vecs):
        row[...] = vec[at : at + 1]
    for at in range(4):
        coming[at].wait()
        there = pl.ds(at * rows, rows)
        go(tok_buf.at[there], tok.at[0, there])
    for at, dst in enumerate((g_up, g_down)):
        coming[4 + at].wait()
        go(mlp_buf.at[at], dst)
    for copy in going:
        copy.wait()


def hand_over(block_out, att, vec, grad_tokens, mlp):
    _, block, f = mlp.shape
    _, rows, d = block_out.shape
    vmem, hbm, anywhere = (pl.BlockSpec(memory_space=space) for space in (pltpu.VMEM, pltpu.HBM, pl.ANY))
    near = [pltpu.with_memory_space_constraint(x, pltpu.VMEM) for x in (block_out, att, vec)]
    far = [pltpu.with_memory_space_constraint(x, pltpu.HBM) for x in (grad_tokens, mlp)]
    shapes = [((block, f), F32), ((block, f), F32), ((block, 3 * d), F32), ((block, d), F32)]
    return pl.pallas_call(
        hand_over_kernel,
        out_shape=[
            *[jax.ShapeDtypeStruct(block_out.shape, LOW)] * 2,
            *[jax.ShapeDtypeStruct(shape, dtype) for shape, dtype in shapes],
            *[jax.ShapeDtypeStruct((1, block), F32)] * 3,
        ],
        in_specs=[vmem] * 3 + [hbm] * 2,
        out_specs=[anywhere] * 6 + [vmem] * 3,
        scratch_shapes=[
            pltpu.VMEM((rows, d), LOW),
            pltpu.VMEM(mlp.shape, F32),
            *[pltpu.VMEM(shape, dtype) for shape, dtype in shapes[2:]],
            pltpu.SemaphoreType.DMA((6,)),
            pltpu.SemaphoreType.DMA((9,)),
        ],
        compiler_params=pltpu.CompilerParams(vmem_limit_bytes=16 * 2**20),
        name="hand_over",
    )(*near, *far)


def local(tokens, key_mask, lengths, routed, w_router, gain_one, gain_two, w_qkv, w_out, w_up, w_down, cotangent):
    _, rows, d = tokens.shape
    n, f = routed.shape[1], w_up.shape[1]
    batch = lax.axis_size("batch")
    s = Sizes(rows, d, n, f, batch)
    found = scratch_of(s)
    vmem, smem, anywhere = (pl.BlockSpec(memory_space=space) for space in (pltpu.VMEM, pltpu.SMEM, pl.ANY))
    shape = pltpu.VMEM if s.folds else jax.ShapeDtypeStruct
    block_out, att, vec, grad_tokens, mlp = pl.pallas_call(
        functools.partial(layer_kernel, s, tuple(found)),
        out_shape=(
            shape(tokens.shape, LOW),
            shape((4, s.pairs, s.block, s.pair), LOW) if s.folds else shape((s.pairs, d, s.pair), F32),
            shape((8, s.block if s.folds else d), F32),
            jax.ShapeDtypeStruct(tokens.shape, LOW),
            jax.ShapeDtypeStruct((2, *s.tail, f), F32),
        ),
        in_specs=[anywhere] * 3 + [smem] + [anywhere] * 8,
        out_specs=[vmem] * 3 + [anywhere] * 2,
        scratch_shapes=list(found.values()),
        compiler_params=pltpu.CompilerParams(collective_id=0, has_side_effects=True, vmem_limit_bytes=VMEM_BYTES),
        name="layer",
    )(
        tokens, cotangent, key_mask, lengths, routed, w_router, gain_one, gain_two, w_qkv, w_out, w_up, w_down,
    )
    if s.folds:
        block_out, grad_tokens, g_up, g_down, g_qkv, g_out, *g_vecs = hand_over(block_out, att, vec, grad_tokens, mlp)
    else:
        mlp = lax.psum_scatter(mlp, "batch", scatter_dimension=1, tiled=True)
        vec = lax.psum_scatter(vec, "batch", scatter_dimension=1, tiled=True)
        att = lax.psum_scatter(att, "batch", scatter_dimension=1, tiled=True).astype(LOW)
        att = lax.all_gather(att, "mp", axis=0).astype(F32)
        att = jnp.transpose(att, (2, 0, 1, 3)).reshape(s.block, 4 * d)
        (g_up, g_down), g_qkv, g_out, g_vecs = mlp, att[:, : 3 * d], att[:, 3 * d :], vec[:3]
    g_router, g_one, g_two = (g.reshape(s.block) for g in g_vecs)
    return block_out, grad_tokens, g_router, g_one, g_two, g_qkv, g_out, g_up, g_down.T


def solution(mesh):
    rows_spec = P(("batch", "mp"), None, None)
    in_specs = (
        rows_spec,
        P(("batch", "mp"), None),
        P(("batch", "mp")),
        P(("batch", "mp"), None),
        P(),
        P(),
        P(),
        P(),
        P(),
        P(None, "mp"),
        P("mp", None),
        rows_spec,
    )
    out_specs = (
        rows_spec,
        rows_spec,
        P("batch"),
        P("batch"),
        P("batch"),
        P("batch", None),
        P("batch", None),
        P("batch", "mp"),
        P("mp", "batch"),
    )
    return jax.shard_map(local, mesh=mesh, in_specs=in_specs, out_specs=out_specs, check_vma=False)
```

```python
import functools
import itertools
import types

import jax
import jax.numpy as jnp
from jax import lax
from jax.experimental import pallas as pl
from jax.experimental.pallas import tpu as pltpu
from jax.sharding import PartitionSpec as P

HEADS = 12
EPSILON = 1e-06
LOW = jnp.bfloat16
F32 = jnp.float32
MESH = pl.DeviceIdType.MESH
VMEM_BYTES = 58 * 2**20
AXES = "dxbay"
MLP_ORDERS = ("yab", "aby", "yab", "aby", "yab", "yab")
ATT_ORDERS = ("dxyabG", "dxyabG", "dxaybG", "daxybG", "dyxab", "dxyabG")
SEQUENCE = (
    ("f0", "f1", "u1", "u0", "t", "w1", "u4", "u5", "w0", "u3", "w5", "r0", "r1", "w3", "r3", "u2", "r2"),
    ("b0", "w2", "m1", "w4", "a0", "b3", "m0", "b1", "m3", "b2", "a1", "a3", "b4", "b5", "o0", "m2", "m5"),
    ("a4", "a2", "a0", "a5", "m4", "m0", "o1", "a1", "e0", "a2", "e1", "a3", "z", "m3", "s6", "m2", "a4"),
    ("v", "a0", "a5", "s4", "m4", "a1", "m5", "a3", "a2", "s3", "a4", "a0", "v", "a5", "a3", "a1", "m1", "a4"),
    ("v", "a2", "m5", "a5", "a0", "s1", "a3", "m3", "a1", "s0", "v", "a4", "a2", "s7", "s5", "a5", "m1", "m0"),
    ("m2", "a0", "s2", "m4", "a1", "a4", "a3", "v", "a2", "a4", "a5"),
)


def mm(a, b, along_a=1, along_b=0):
    return lax.dot_general(a, b, (((along_a,), (along_b,)), ((), ())), preferred_element_type=F32)


def norm_rate(v):
    return lax.rsqrt(jnp.mean(v * v, axis=1, keepdims=True) + EPSILON)


def gelu_and_slope(v):
    c = 0.7978845608028654
    square = v * v
    t = jnp.tanh(v * (c + (c * 0.044715) * square))
    half = 0.5 + 0.5 * t
    slope = half + (0.5 * v) * (1.0 - t * t) * (c + (c * 3 * 0.044715) * square)
    return v * half, slope


def iota(shape, dim):
    return lax.broadcasted_iota(jnp.int32, shape, dim)


class Sizes:
    def __init__(self, rows, width, slots, hidden, batch):
        self.rows, self.width, self.slots, self.hidden, self.batch = rows, width, slots, hidden, batch
        self.block = width // batch
        self.folds = batch == 8 and self.block % 16 == 0
        self.pair = 2 * (width // HEADS)
        self.pairs = HEADS // 2
        self.part = hidden // 3
        self.half, self.work = slots // 2, slots * 3 // 4
        self.spill = slots - self.work
        self.mlp_orders = MLP_ORDERS if self.folds else ("",) * len(MLP_ORDERS)
        self.att_orders = ATT_ORDERS if self.folds else ("dx",) * len(ATT_ORDERS)
        self.tail = (self.block,) if self.folds else (width,)

    def table(self, axes, columns):
        return (*(2 for axis in AXES if axis in axes), *self.tail, columns)


def scratch_of(s):
    n, d, f = s.slots, s.width, s.hidden
    found = dict(
        cot=pltpu.VMEM((s.rows, d), LOW),
        wqkv=pltpu.VMEM((d, 3 * d), LOW),
        wout=pltpu.VMEM((d, d), LOW),
        wup=pltpu.VMEM((2, d, f), LOW),
        wdn=pltpu.VMEM((2, f, d), LOW),
        wout_t=pltpu.VMEM((d, d), LOW),
        wup_t=pltpu.VMEM((2, f, d), LOW),
        wdn_t=pltpu.VMEM((2, d, f), LOW),
        pick=pltpu.VMEM((n, s.rows), LOW),
        picked=pltpu.VMEM((n, d), F32),
        cotr=pltpu.VMEM((n, d), LOW),
        first=pltpu.VMEM((n, d), LOW),
        qkv=pltpu.VMEM((n, 3 * d), LOW),
        bias=pltpu.VMEM((n, n), F32),
        probs=pltpu.VMEM((HEADS, n, n), LOW),
        mixed=pltpu.VMEM((n, d), LOW),
        first_t=pltpu.VMEM((d, n), LOW),
        mixed_t=pltpu.VMEM((d, n), LOW),
        sec_t=pltpu.VMEM((d, 2 * s.work), LOW),
        gm_t=pltpu.VMEM((d, 2 * s.work), LOW),
        upd_out=pltpu.VMEM((n, d), LOW),
        upd_tok=pltpu.VMEM((n, d), LOW),
        attended=pltpu.VMEM((n, d), F32),
        resid=pltpu.VMEM((n, d), F32),
        sec=pltpu.VMEM((2 * s.work, d), LOW),
        gm=pltpu.VMEM((2 * s.work, d), LOW),
        act=pltpu.VMEM((2, 2 * s.work, f), LOW),
        gpre=pltpu.VMEM((2, 2 * s.work, f), LOW),
        gs_own=pltpu.VMEM((s.work, d), F32),
        mo_own=pltpu.VMEM((s.work, d), F32),
        gs_out=pltpu.VMEM((s.work, d), LOW),
        mo_out=pltpu.VMEM((s.work, d), LOW),
        gs_in=pltpu.VMEM((s.work, d), LOW),
        mo_in=pltpu.VMEM((s.work, d), LOW),
        spill_out=pltpu.VMEM((4, s.spill, d), LOW),
        spill_in=pltpu.VMEM((5, s.spill, d), LOW),
        mo=pltpu.VMEM((n, d), F32),
        mask_row=pltpu.VMEM((1, s.rows), jnp.int32),
        wanted_row=pltpu.VMEM((1, n), jnp.int32),
        gres=pltpu.VMEM((n, d), F32),
        gfirst=pltpu.VMEM((n, d), F32),
        gatt=pltpu.VMEM((n, d), LOW),
        gmix=pltpu.VMEM((n, d), LOW),
        dqkv=pltpu.VMEM((n, 3 * d), LOW),
        vec=pltpu.VMEM((6, 8, d), F32),
        vec_in=pltpu.VMEM((5, 8, d), F32),
        send_sem=pltpu.SemaphoreType.DMA((112,)),
        recv_sem=pltpu.SemaphoreType.DMA((112,)),
        summed=pltpu.VMEM((2, *s.tail, f), F32),
        router=pltpu.VMEM((d,), LOW),
        one=pltpu.VMEM((d,), LOW),
        two=pltpu.VMEM((d,), LOW),
        write_sem=pltpu.SemaphoreType.DMA((12,)),
        local_sem=pltpu.SemaphoreType.DMA((24,)),
    )
    batch_axes = "bay" if s.folds else ""
    for name, orders, axes, columns in (("m", s.mlp_orders, batch_axes, s.part), ("a", s.att_orders, "dx" + batch_axes, s.pair)):
        for at, order in enumerate(orders):
            left = axes
            found[f"{name}{at}_0"] = pltpu.VMEM(s.table(left, columns), LOW)
            for step, axis in enumerate(order.strip("G")):
                left = left.replace(axis, "")
                found[f"{name}{at}_{step + 1}"] = pltpu.VMEM(s.table(left, columns), LOW)
            if name == "m":
                found[f"u{at}"] = pltpu.VMEM(s.table(axes, columns), LOW)
    if s.folds:
        found["gathered"] = pltpu.VMEM((4, s.pairs, s.block, s.pair), LOW)
    return found


def layer_kernel(s, names, *refs):
    ins, outs, scratch = refs[:12], refs[12:17], refs[17:]
    tokens, cotangent, key_mask, lengths, routed, w_router, gain_one, gain_two, w_qkv, w_out, w_up, w_down = ins
    block_out, o_att, o_vec, grad_tokens, o_mlp = outs
    v = types.SimpleNamespace(**dict(zip(names, scratch, strict=True)), tok=block_out.at[0])
    n, d, f, pair = s.slots, s.width, s.hidden, s.pair
    half_rows = n // 2

    b, m = lax.axis_index("batch"), lax.axis_index("mp")
    lo, hi = m % 2, m // 2
    y = b % 2
    here = {"d": lo, "x": hi, "y": y}
    other_m = {"d": m + 1 - 2 * lo, "x": m + 2 - 4 * hi, "f": 3 - m}
    peer = {axis: (b, to) for axis, to in other_m.items()} | {"y": (b + 1 - 2 * y, m), "q": (b + 1 - 2 * y, other_m["x"])}
    if s.folds:
        zl, zh = (b // 2) % 2, b // 4
        here |= {"a": zl, "b": zh}
        peer |= {"a": (b + 2 - 4 * zl, m), "b": (b + 4 - 8 * zh, m)}

    barrier = pltpu.get_barrier_semaphore()
    for other in peer.values():
        pl.semaphore_signal(barrier, inc=1, device_id=other, device_id_type=MESH)

    sent = []

    def send(src, dst, axis):
        at = len(sent)
        copy = pltpu.make_async_remote_copy(
            src_ref=src,
            dst_ref=dst,
            send_sem=v.send_sem.at[at],
            recv_sem=v.recv_sem.at[at],
            device_id=peer[axis],
            device_id_type=MESH,
        )
        copy.start()
        sent.append(copy)
        return copy

    fetches = []

    def fetch(src, dst):
        fetches.append(pltpu.make_async_copy(src, dst, v.local_sem.at[len(fetches)]))
        fetches[-1].start()
        return fetches[-1]

    writes, stored = [], []

    def write(src, dst):
        writes.append(pltpu.make_async_copy(src, dst, v.write_sem.at[len(writes)]))
        writes[-1].start()

    quarter = s.rows // 4
    quarters = [pl.ds(at * quarter, quarter) for at in range(4)]
    got_wanted = fetch(routed, v.wanted_row)
    got_rows = [fetch(src, dst) for src, dst in ((w_router, v.router), (gain_one, v.one), (gain_two, v.two))]
    got_tok = [fetch(tokens.at[0, there], v.tok.at[there]) for there in quarters]
    got_cot = [fetch(cotangent.at[0, there], v.cot.at[there]) for there in quarters]
    got_mask = fetch(key_mask, v.mask_row)

    got_wanted.wait()
    live_count = lengths[0] // 8
    wanted = jnp.where(iota((1, n), 1) < live_count, v.wanted_row[...], -1).astype(F32)
    on_diagonal = iota((n, n), 0) == iota((n, n), 1)
    wanted_column = jnp.sum(jnp.where(on_diagonal, wanted, 0.0), axis=1, keepdims=True).astype(jnp.int32)
    live = jnp.where(iota((n, 1), 0) < live_count, 1.0, 0.0)
    v.pick[...] = jnp.where(iota((n, s.rows), 1) == wanted_column, 1.0, 0.0).astype(LOW)

    def gather(table, got):
        total = 0.0
        for at in range(4):
            got[at].wait()
            cols = slice(at * quarter, (at + 1) * quarter)
            total = total + mm(v.pick[:, cols], table[cols])
        return total

    picked = gather(v.tok, got_tok)
    v.picked[...] = picked
    for got in got_rows:
        got.wait()
    router_row, one_row, two_row = (row[...].astype(F32).reshape(1, d) for row in (v.router, v.one, v.two))
    gate_rate = 1.0 / (1.0 + jnp.exp(-jnp.sum(picked * router_row, axis=1, keepdims=True)))
    route_gain = live * gate_rate

    got_qkv = fetch(w_qkv, v.wqkv)
    cot_rows = gather(v.cot, got_cot)
    got_out = fetch(w_out, v.wout)
    got_up = fetch(w_up, v.wup.at[0])
    got_down = fetch(w_down, v.wdn.at[0])
    half, work, spill = s.half, s.work, s.spill
    mine_a, other_a = pl.ds(0, half), pl.ds(half, half)
    mine_b, other_b = pl.ds(2 * half, spill), pl.ds(2 * half + spill, spill)
    gm = (route_gain * cot_rows).astype(LOW)
    v.gm[0:half] = gm[:half]
    v.spill_out[0] = gm[work:]

    pl.semaphore_wait(barrier, len(peer))
    sent_gm = [send(v.gm.at[mine_a], v.gm.at[other_a], "x")]
    spilt_gm = send(v.spill_out.at[0], v.spill_in.at[0], "y")
    sent_up = send(w_up, v.wup.at[1], "d")
    sent_down = send(w_down, v.wdn.at[1], "d")

    v.cotr[...] = cot_rows.astype(LOW)
    rate_one = norm_rate(picked)
    v.first[...] = (picked * rate_one * one_row).astype(LOW)
    got_qkv.wait()
    for at in range(0, 3 * d, 256):
        v.qkv[:, at : at + 256] = mm(v.first[...], v.wqkv[:, at : at + 256]).astype(LOW)

    place_spill = jnp.where(iota((spill, spill), 0) + half - live_count == iota((spill, spill), 1), 1.0, 0.0).astype(LOW)
    live_b = live[half:work]

    def merge(own, arrived):
        return (own.astype(F32) * live_b + mm(place_spill, arrived)).astype(LOW)

    def part_back(merged):
        return mm(place_spill, merged, 0, 0).astype(LOW)

    peer_live = 2 * work - live_count
    place_peer = jnp.where(iota((spill, spill), 0) + half - peer_live == iota((spill, spill), 1), 1.0, 0.0).astype(LOW)

    spilt_gm.wait_recv()
    v.gm[2 * half : 2 * half + spill] = merge(gm[half:work], v.spill_in[0])
    sent_gm.append(send(v.gm.at[mine_b], v.gm.at[other_b], "x"))

    got_mask.wait()
    mask_rows = jnp.broadcast_to(v.mask_row[...].astype(F32), (8, s.rows)).astype(LOW)
    key_open = mm(mask_rows, v.pick[...], 1, 1)[0:1] > 0.5
    earlier = iota((n, n), 1) < iota((n, n), 0)
    v.bias[...] = jnp.where((earlier & key_open) | on_diagonal, 0.0, -1e30)

    lane = iota((n, pair), 1)
    side = [lane < pair // 2, lane >= pair // 2]

    def only(x, at):
        return jnp.where(side[at], x.astype(F32), 0.0).astype(LOW)

    for p in range(s.pairs):
        q, k, val = (v.qkv[:, g * d + p * pair : g * d + (p + 1) * pair] for g in range(3))
        q = (q.astype(F32) * (d // HEADS) ** -0.5).astype(LOW)
        total = 0.0
        for h in range(2):
            scores = mm(only(q, h), k, 1, 1) + v.bias[...]
            powers = jnp.exp(scores - jnp.max(scores, axis=1, keepdims=True))
            probs = (powers * (1.0 / jnp.sum(powers, axis=1, keepdims=True))).astype(LOW)
            v.probs[2 * p + h] = probs
            total = total + mm(probs, only(val, h))
        v.mixed[:, p * pair : (p + 1) * pair] = total.astype(LOW)

    got_out.wait()

    def second(start, stop):
        rows = slice(start, stop)
        attended = mm(v.mixed[rows], v.wout[...])
        v.attended[rows] = attended
        resid = v.picked[rows] + attended
        v.resid[rows] = resid
        return (resid * norm_rate(resid) * two_row).astype(LOW)

    normed = second(0, n)
    v.spill_out[1] = normed[work:]
    spilt_sec = send(v.spill_out.at[1], v.spill_in.at[1], "y")
    v.sec[0:half] = normed[:half]
    sent_sec = [send(v.sec.at[mine_a], v.sec.at[other_a], "x")]
    second_b = normed[half:work]

    def feed(start, count):
        rows = slice(start, start + count)
        x, g = v.sec[rows], v.gm[rows]
        gs = 0.0
        for w in range(2):
            act, slope = gelu_and_slope(mm(x, v.wup[w]))
            v.act[w, rows] = act.astype(LOW)
            gpre = (mm(g, v.wdn_t[w]) * slope).astype(LOW)
            v.gpre[w, rows] = gpre
            gs = gs + mm(gpre, v.wup_t[w])
        return gs

    def feed_out(start, count):
        rows = slice(start, start + count)
        return mm(v.act[0, rows], v.wdn[0]) + mm(v.act[1, rows], v.wdn[1])

    got_up.wait()
    got_down.wait()
    sent_up.wait_recv()
    sent_down.wait_recv()
    for w in range(2):
        v.wup_t[w] = v.wup[w].T
        v.wdn_t[w] = v.wdn[w].T
    v.gs_own[0:half] = feed(0, half)
    spilt_sec.wait_recv()
    v.sec[2 * half : 2 * half + spill] = merge(second_b, v.spill_in[1])
    sent_sec.append(send(v.sec.at[mine_b], v.sec.at[other_b], "x"))
    gs = feed(2 * half, spill)
    v.gs_own[half:work] = gs
    v.spill_out[2] = gs.astype(LOW)
    spilt_own = send(v.spill_out.at[2], v.spill_in.at[2], "y")
    v.mo_own[0:half] = feed_out(0, half)
    v.mo_own[half:work] = feed_out(2 * half, spill)
    v.sec_t[:, :half] = v.sec[0:half].T
    v.gm_t[:, :half] = v.gm[0:half].T
    for copy in sent_gm:
        copy.wait_recv()
    v.gm_t[:, half:] = v.gm[half:].T
    sent_gs, sent_mo, spilt = [], [], {}

    def transposes():
        v.wout_t[...] = v.wout[...].T
        v.first_t[...] = v.first[...].T
        v.mixed_t[...] = v.mixed[...].T

    def send_back(out, into, start, count):
        there = pl.ds(start, count)
        return send(out.at[there], into.at[there], "x")

    def feed_other(at):
        sent_sec[at].wait_recv()
        start, count, into = (half, half, 0) if at == 0 else (2 * half + spill, spill, half)
        rows = slice(into, into + count)
        v.gs_out[rows] = feed(start, count).astype(LOW)
        if at == 0:
            sent_gs.append(send_back(v.gs_out, v.gs_in, 0, half // 2))
        else:
            sent_gs.append(send_back(v.gs_out, v.gs_in, half, spill))
            spilt["gs"] = send(v.gs_out.at[pl.ds(half, spill)], v.spill_in.at[4], "q")
            sent_gs.append(send_back(v.gs_out, v.gs_in, half // 2, half // 2))
        v.mo_out[rows] = feed_out(start, count).astype(LOW)
        if at == 1:
            sent_mo.append(send_back(v.mo_out, v.mo_in, half, spill))
            sent_mo.append(send_back(v.mo_out, v.mo_in, 0, half))
            v.sec_t[:, half:] = v.sec[half:].T

    def weight_grad(at, w):
        left, right = (v.sec_t, v.gpre) if at < 3 else (v.gm_t, v.act)
        cols = slice(at % 3 * s.part, (at % 3 + 1) * s.part)
        return mm(left[...], right[w, :, cols])

    sent_core = {}

    def other_core(at):
        table = getattr(v, f"u{at}")
        table[...] = weight_grad(at, 1).astype(LOW).reshape(table.shape)
        sent_core[at] = send(table, getattr(v, f"m{at}_0"), "d")

    class Sum:
        def __init__(self, name, axes, order, finish):
            self.name, self.axes, self.order, self.finish, self.at = name, axes, order, finish, 0
            if order:
                self.start()

        def table(self, at):
            return getattr(v, f"{self.name}_{at}")

        def start(self):
            axis = self.order[self.at]
            src = self.table(self.at).at[tuple(1 - here[k] if k == axis else slice(None) for k in self.axes)]
            self.going = send(src, self.table(self.at + 1), axis)

        def advance(self):
            if self.at == len(self.order):
                self.finish.advance()
                return
            axis = self.order[self.at]
            self.going.wait_recv()
            kept, arrived = self.table(self.at), self.table(self.at + 1)
            last = self.at + 1 == len(self.order)
            rest = self.axes.replace(axis, "")
            for index in itertools.product(*[range(2)] * len(rest)):
                full = dict(zip(rest, index, strict=True)) | {axis: here[axis]}
                total = arrived[index].astype(F32) + kept[tuple(full[k] for k in self.axes)].astype(F32)
                if last:
                    self.finish.begin(total)
                else:
                    arrived[index] = total.astype(LOW)
            self.axes, self.at = rest, self.at + 1
            if not last:
                self.start()

    class Store:
        def __init__(self, at):
            self.at = at

        def begin(self, total):
            kind, cols = self.at // 3, slice(self.at % 3 * s.part, (self.at % 3 + 1) * s.part)
            v.summed[kind, :, cols] = total
            stored.append(self.at)
            if all(3 * kind + at in stored for at in range(3)):
                write(v.summed.at[kind], o_mlp.at[kind])

    class Gather:
        def __init__(self, p, direct):
            self.p, self.direct = p, direct

        def begin(self, total):
            if not s.folds:
                o_att[self.p] = total
                return
            piece = v.gathered.at[m, self.p]
            piece[...] = total.astype(LOW)
            self.over_x = send(piece, piece, "x")
            self.others = [send(piece, piece, "d")]
            if self.direct:
                self.others.append(send(piece, piece, "f"))
            self.handed_on = self.direct

        def advance(self):
            if not self.handed_on:
                self.over_x.wait_recv()
                piece = v.gathered.at[other_m["x"], self.p]
                self.others.append(send(piece, piece, "d"))
                self.handed_on = True
                return
            if self.direct:
                self.over_x.wait_recv()
            for copy in self.others:
                copy.wait_recv()
            for g in range(4):
                o_att[g, self.p] = v.gathered[g, self.p]

    sums = {}

    def own_core(at):
        own = weight_grad(at, 0)
        sent_core[at].wait_recv()
        table = getattr(v, f"m{at}_0")
        table[...] = (table[...].astype(F32) + own.reshape(table.shape)).astype(LOW)
        if s.folds:
            sums[f"m{at}"] = Sum(f"m{at}", "bay", s.mlp_orders[at], Store(at))
        else:
            v.summed[at // 3, :, at % 3 * s.part : (at % 3 + 1) * s.part] = table[...].astype(F32)
            if at % 3 == 2:
                write(v.summed.at[at // 3], o_mlp.at[at // 3])

    gain_two_sums = []

    def second_back(at):
        if at < 3:
            start, stop = ((0, half // 2), (half, work), (half // 2, half))[at]
            sent_gs[at].wait_recv()
            gs = (v.gs_own[start:stop] + v.gs_in[start:stop].astype(F32)).astype(LOW)
            if at == 1:
                gs = gs.astype(F32) * live_b
        else:
            start, stop = work, n
            spilt_own.wait_recv()
            spilt["gs"].wait_recv()
            gs = mm(place_peer, (v.spill_in[2].astype(F32) + v.spill_in[4].astype(F32)).astype(LOW), 0, 0)
        rows = slice(start, stop)
        gs = gs.astype(F32)
        resid = v.resid[rows]
        rate = norm_rate(resid)
        gain_two_sums.append(jnp.sum(gs * (resid * rate), axis=0, keepdims=True))
        scaled = gs * two_row
        gres = rate * scaled - resid * (rate * rate * rate * jnp.mean(scaled * resid, axis=1, keepdims=True))
        v.gres[rows] = gres
        gatt = (route_gain[rows] * v.cotr[rows].astype(F32) + gres).astype(LOW)
        v.gatt[rows] = gatt
        v.gmix[rows] = mm(gatt, v.wout_t[...]).astype(LOW)

    def part_mo(at):
        if at == 0:
            sent_mo[0].wait_recv()
            mo = (v.mo_own[half:work] + v.mo_in[half:work].astype(F32)).astype(LOW)
            v.spill_out[3] = part_back(mo)
            spilt["mo"] = send(v.spill_out.at[3], v.spill_in.at[3], "y")
            v.mo[half:work] = mo.astype(F32)
        else:
            sent_mo[1].wait_recv()
            v.mo[0:half] = (v.mo_own[0:half] + v.mo_in[0:half].astype(F32)).astype(LOW).astype(F32)
            spilt["mo"].wait_recv()
            v.mo[work:n] = v.spill_in[3].astype(F32)

    def attend_back(p):
        where = [slice(g * d + p * pair, g * d + (p + 1) * pair) for g in range(3)]
        q, k, val = (v.qkv[:, cols] for cols in where)
        gmix = v.gmix[:, p * pair : (p + 1) * pair]
        gq, gk, gv = 0.0, 0.0, 0.0
        for h in range(2):
            probs = v.probs[2 * p + h]
            gmix_h = only(gmix, h)
            gprobs = mm(gmix_h, val, 1, 1)
            wide = probs.astype(F32)
            product = gprobs * wide
            gscores = product - wide * jnp.sum(product, axis=1, keepdims=True)
            gscores = (gscores * (d // HEADS) ** -0.5).astype(LOW)
            gq = gq + mm(gscores, only(k, h))
            gk = gk + mm(gscores, only(q, h), 0, 0)
            gv = gv + mm(probs, gmix_h, 0, 0)
        table = getattr(v, f"a{p}_0")
        lower = []
        for cols, grad in zip(where, (gq, gk, gv), strict=True):
            lower.append(grad.astype(LOW))
            v.dqkv[:, cols] = lower[-1]
        both = mm(v.first_t[...], jnp.concatenate(lower[:2], axis=1)).astype(LOW)
        shape = table.shape[2:]
        table[0, 0] = both[:, :pair].reshape(shape)
        table[1, 0] = both[:, pair:].reshape(shape)
        table[0, 1] = mm(v.first_t[...], lower[2]).astype(LOW).reshape(shape)
        table[1, 1] = mm(v.mixed_t[...], v.gatt[:, p * pair : (p + 1) * pair]).astype(LOW).reshape(shape)
        order = s.att_orders[p]
        sums[f"a{p}"] = Sum(f"a{p}", "dxbay" if s.folds else "dx", order.strip("G"), Gather(p, "G" in order))

    kept = {}

    def first_back(at):
        if at == 0:
            v.gfirst[...] = mm(v.dqkv[...], v.wqkv[...], 1, 1)
            return
        gfirst, picked, rate = v.gfirst[...], v.picked[...], rate_one
        kept["gain_one"] = jnp.sum(gfirst * (picked * rate), axis=0, keepdims=True)
        scaled = gfirst * one_row
        gnorm = rate * scaled - picked * (rate * rate * rate * jnp.mean(scaled * picked, axis=1, keepdims=True))
        v.gres[...] = v.gres[...] + gnorm

    def finish_rows():
        picked = v.picked[...]
        branch = v.attended[...] + v.mo[...]
        grate = live * jnp.sum(v.cotr[...].astype(F32) * branch, axis=1, keepdims=True)
        glogit = grate * gate_rate * (1.0 - gate_rate)
        router_sum = jnp.sum(glogit * picked, axis=0, keepdims=True)
        v.upd_out[...] = (route_gain * branch).astype(LOW)
        v.upd_tok[...] = (live * (v.gres[...] + glogit * router_row)).astype(LOW)
        row = iota((8, d), 0)
        gain_two_sum = sum(gain_two_sums)
        v.vec[0] = jnp.where(row == 0, router_sum, jnp.where(row == 1, kept["gain_one"], jnp.where(row == 2, gain_two_sum, 0.0)))
        sums["v"] = Everywhere("dxyab" if s.folds else "dx")

    tile = s.rows // 8

    def spread(at):
        rows = slice(at * tile, (at + 1) * tile)
        there = pl.ds(at * tile, tile)
        place = jnp.where(iota((tile, n), 0) + at * tile == wanted.astype(jnp.int32), 1.0, 0.0).astype(LOW)
        for table, update in ((v.tok, v.upd_out), (v.cot, v.upd_tok)):
            table[rows] = (table[rows].astype(F32) + mm(place, update[...])).astype(LOW)
        write(v.cot.at[there], grad_tokens.at[0, there])

    class Everywhere:
        def __init__(self, order):
            self.order, self.at = order, 0
            self.start()

        def start(self):
            self.going = send(v.vec.at[self.at], v.vec_in.at[self.at], self.order[self.at])

        def advance(self):
            self.going.wait_recv()
            v.vec[self.at + 1] = v.vec[self.at] + v.vec_in[self.at]
            self.at += 1
            if self.at < len(self.order):
                self.start()
            else:
                total = v.vec[self.at]
                if not s.folds:
                    o_vec[...] = total
                    return
                mine = iota((d, s.block), 0) == iota((d, s.block), 1) + b * s.block
                o_vec[...] = lax.dot_general(
                    total, jnp.where(mine, 1.0, 0.0), (((1,), (0,)), ((), ())),
                    preferred_element_type=F32, precision=lax.Precision.HIGHEST,
                )

    steps = {"f": feed_other, "u": other_core, "w": own_core, "r": second_back, "b": attend_back, "s": spread, "o": part_mo, "e": first_back}
    for step in itertools.chain(*SEQUENCE):
        if step[0] in steps:
            steps[step[0]](int(step[1:]))
        elif step == "t":
            transposes()
        elif step == "z":
            finish_rows()
        elif s.folds:
            sums[step].advance()
    if not s.folds:
        for name, total in sums.items():
            total.advance()
            total.advance()
    for copy in sent:
        copy.wait_send()
    for copy in writes:
        copy.wait()


def hand_over_kernel(block_out, att, vec, grad_tokens, mlp, out, tok, g_up, g_down, g_qkv, g_out, *rest):
    *vecs, tok_buf, mlp_buf, qkv_buf, out_buf, come_sem, go_sem = rest
    _, pairs, _, pair = att.shape
    d = g_out.shape[1]
    rows = tok.shape[1] // 4
    going = []

    def go(src, dst):
        going.append(pltpu.make_async_copy(src, dst, go_sem.at[len(going)]))
        going[-1].start()

    coming = []
    for src, dst in (
        *[(grad_tokens.at[0, pl.ds(at * rows, rows)], tok_buf.at[pl.ds(at * rows, rows)]) for at in range(4)],
        *[(mlp.at[at], mlp_buf.at[at]) for at in range(2)],
    ):
        coming.append(pltpu.make_async_copy(src, dst, come_sem.at[len(coming)]))
        coming[-1].start()
    go(block_out, out)
    for p in range(pairs):
        for g in range(3):
            qkv_buf[:, g * d + p * pair : g * d + (p + 1) * pair] = att[g, p].astype(F32)
        out_buf[:, p * pair : (p + 1) * pair] = att[3, p].astype(F32)
    go(qkv_buf, g_qkv)
    go(out_buf, g_out)
    for at, row in enumerate(vecs):
        row[...] = vec[at : at + 1]
    for at in range(4):
        coming[at].wait()
        there = pl.ds(at * rows, rows)
        go(tok_buf.at[there], tok.at[0, there])
    for at, dst in enumerate((g_up, g_down)):
        coming[4 + at].wait()
        go(mlp_buf.at[at], dst)
    for copy in going:
        copy.wait()


def hand_over(block_out, att, vec, grad_tokens, mlp):
    _, block, f = mlp.shape
    _, rows, d = block_out.shape
    vmem, hbm, anywhere = (pl.BlockSpec(memory_space=space) for space in (pltpu.VMEM, pltpu.HBM, pl.ANY))
    near = [pltpu.with_memory_space_constraint(x, pltpu.VMEM) for x in (block_out, att, vec)]
    far = [pltpu.with_memory_space_constraint(x, pltpu.HBM) for x in (grad_tokens, mlp)]
    shapes = [((block, f), F32), ((block, f), F32), ((block, 3 * d), F32), ((block, d), F32)]
    return pl.pallas_call(
        hand_over_kernel,
        out_shape=[
            *[jax.ShapeDtypeStruct(block_out.shape, LOW)] * 2,
            *[jax.ShapeDtypeStruct(shape, dtype) for shape, dtype in shapes],
            *[jax.ShapeDtypeStruct((1, block), F32)] * 3,
        ],
        in_specs=[vmem] * 3 + [hbm] * 2,
        out_specs=[anywhere] * 6 + [vmem] * 3,
        scratch_shapes=[
            pltpu.VMEM((rows, d), LOW),
            pltpu.VMEM(mlp.shape, F32),
            *[pltpu.VMEM(shape, dtype) for shape, dtype in shapes[2:]],
            pltpu.SemaphoreType.DMA((6,)),
            pltpu.SemaphoreType.DMA((9,)),
        ],
        compiler_params=pltpu.CompilerParams(vmem_limit_bytes=16 * 2**20),
        name="hand_over",
    )(*near, *far)


def local(tokens, key_mask, lengths, routed, w_router, gain_one, gain_two, w_qkv, w_out, w_up, w_down, cotangent):
    _, rows, d = tokens.shape
    n, f = routed.shape[1], w_up.shape[1]
    batch = lax.axis_size("batch")
    s = Sizes(rows, d, n, f, batch)
    found = scratch_of(s)
    vmem, smem, anywhere = (pl.BlockSpec(memory_space=space) for space in (pltpu.VMEM, pltpu.SMEM, pl.ANY))
    shape = pltpu.VMEM if s.folds else jax.ShapeDtypeStruct
    block_out, att, vec, grad_tokens, mlp = pl.pallas_call(
        functools.partial(layer_kernel, s, tuple(found)),
        out_shape=(
            shape(tokens.shape, LOW),
            shape((4, s.pairs, s.block, s.pair), LOW) if s.folds else shape((s.pairs, d, s.pair), F32),
            shape((8, s.block if s.folds else d), F32),
            jax.ShapeDtypeStruct(tokens.shape, LOW),
            jax.ShapeDtypeStruct((2, *s.tail, f), F32),
        ),
        in_specs=[anywhere] * 3 + [smem] + [anywhere] * 8,
        out_specs=[vmem] * 3 + [anywhere] * 2,
        scratch_shapes=list(found.values()),
        compiler_params=pltpu.CompilerParams(collective_id=0, has_side_effects=True, vmem_limit_bytes=VMEM_BYTES),
        name="layer",
    )(
        tokens, cotangent, key_mask, lengths, routed, w_router, gain_one, gain_two, w_qkv, w_out, w_up, w_down,
    )
    if s.folds:
        block_out, grad_tokens, g_up, g_down, g_qkv, g_out, *g_vecs = hand_over(block_out, att, vec, grad_tokens, mlp)
    else:
        mlp = lax.psum_scatter(mlp, "batch", scatter_dimension=1, tiled=True)
        vec = lax.psum_scatter(vec, "batch", scatter_dimension=1, tiled=True)
        att = lax.psum_scatter(att, "batch", scatter_dimension=1, tiled=True).astype(LOW)
        att = lax.all_gather(att, "mp", axis=0).astype(F32)
        att = jnp.transpose(att, (2, 0, 1, 3)).reshape(s.block, 4 * d)
        (g_up, g_down), g_qkv, g_out, g_vecs = mlp, att[:, : 3 * d], att[:, 3 * d :], vec[:3]
    g_router, g_one, g_two = (g.reshape(s.block) for g in g_vecs)
    return block_out, grad_tokens, g_router, g_one, g_two, g_qkv, g_out, g_up, g_down.T


def solution(mesh):
    rows_spec = P(("batch", "mp"), None, None)
    in_specs = (
        rows_spec,
        P(("batch", "mp"), None),
        P(("batch", "mp")),
        P(("batch", "mp"), None),
        P(),
        P(),
        P(),
        P(),
        P(),
        P(None, "mp"),
        P("mp", None),
        rows_spec,
    )
    out_specs = (
        rows_spec,
        rows_spec,
        P("batch"),
        P("batch"),
        P("batch"),
        P("batch", None),
        P("batch", None),
        P("batch", "mp"),
        P("mp", "batch"),
    )
    return jax.shard_map(local, mesh=mesh, in_specs=in_specs, out_specs=out_specs, check_vma=False)
```

```python
import functools
import itertools
import types

import jax
import jax.numpy as jnp
from jax import lax
from jax.experimental import pallas as pl
from jax.experimental.pallas import tpu as pltpu
from jax.sharding import PartitionSpec as P

HEADS = 12
EPSILON = 1e-06
LOW = jnp.bfloat16
F32 = jnp.float32
MESH = pl.DeviceIdType.MESH
VMEM_BYTES = 58 * 2**20
AXES = "dxbay"
MLP_ORDERS = ("yab", "aby", "yab", "aby", "yab", "yab")
ATT_ORDERS = ("dxyabG", "dxyabG", "dxaybG", "daxybG", "dyxab", "dxyabG")
SEQUENCE = (
    ("f0", "f1", "u1", "u0", "t", "w1", "u4", "u5", "w0", "u3", "w5", "r0", "r1", "w3", "r3", "u2", "r2"),
    ("b0", "w2", "m1", "w4", "a0", "b3", "m0", "b1", "m3", "b2", "a1", "a3", "b4", "b5", "o0", "m2", "m5"),
    ("a4", "a2", "a0", "a5", "m4", "m0", "o1", "a1", "e0", "a2", "e1", "a3", "z", "m3", "s6", "m2", "a4"),
    ("v", "a0", "a5", "s4", "m4", "a1", "m5", "a3", "a2", "s3", "a4", "a0", "v", "a5", "a3", "a1", "m1", "a4"),
    ("v", "a2", "m5", "a5", "a0", "s1", "a3", "m3", "a1", "s0", "v", "a4", "a2", "s7", "s5", "a5", "m1", "m0"),
    ("m2", "a0", "s2", "m4", "a1", "a4", "a3", "v", "a2", "a4", "a5"),
)


def mm(a, b, along_a=1, along_b=0):
    return lax.dot_general(a, b, (((along_a,), (along_b,)), ((), ())), preferred_element_type=F32)


def norm_rate(v):
    return lax.rsqrt(jnp.mean(v * v, axis=1, keepdims=True) + EPSILON)


def gelu_and_slope(v):
    c = 0.7978845608028654
    square = v * v
    t = jnp.tanh(v * (c + (c * 0.044715) * square))
    half = 0.5 + 0.5 * t
    slope = half + (0.5 * v) * (1.0 - t * t) * (c + (c * 3 * 0.044715) * square)
    return v * half, slope


def iota(shape, dim):
    return lax.broadcasted_iota(jnp.int32, shape, dim)


class Sizes:
    def __init__(self, rows, width, slots, hidden, batch):
        self.rows, self.width, self.slots, self.hidden, self.batch = rows, width, slots, hidden, batch
        self.block = width // batch
        self.folds = batch == 8 and self.block % 16 == 0
        self.pair = 2 * (width // HEADS)
        self.pairs = HEADS // 2
        self.part = hidden // 3
        self.half, self.work = slots // 2, slots * 3 // 4
        self.spill = slots - self.work
        self.mlp_orders = MLP_ORDERS if self.folds else ("",) * len(MLP_ORDERS)
        self.att_orders = ATT_ORDERS if self.folds else ("dx",) * len(ATT_ORDERS)
        self.tail = (self.block,) if self.folds else (width,)

    def table(self, axes, columns):
        return (*(2 for axis in AXES if axis in axes), *self.tail, columns)


def scratch_of(s):
    n, d, f = s.slots, s.width, s.hidden
    found = dict(
        cot=pltpu.VMEM((s.rows, d), LOW),
        wqkv=pltpu.VMEM((d, 3 * d), LOW),
        wout=pltpu.VMEM((d, d), LOW),
        wup=pltpu.VMEM((2, d, f), LOW),
        wdn=pltpu.VMEM((2, f, d), LOW),
        wout_t=pltpu.VMEM((d, d), LOW),
        wup_t=pltpu.VMEM((2, f, d), LOW),
        wdn_t=pltpu.VMEM((2, d, f), LOW),
        pick=pltpu.VMEM((n, s.rows), LOW),
        picked=pltpu.VMEM((n, d), F32),
        cotr=pltpu.VMEM((n, d), LOW),
        first=pltpu.VMEM((n, d), LOW),
        qkv=pltpu.VMEM((n, 3 * d), LOW),
        bias=pltpu.VMEM((n, n), F32),
        probs=pltpu.VMEM((HEADS, n, n), LOW),
        mixed=pltpu.VMEM((n, d), LOW),
        first_t=pltpu.VMEM((d, n), LOW),
        mixed_t=pltpu.VMEM((d, n), LOW),
        sec_t=pltpu.VMEM((d, 2 * s.work), LOW),
        gm_t=pltpu.VMEM((d, 2 * s.work), LOW),
        upd_out=pltpu.VMEM((n, d), LOW),
        upd_tok=pltpu.VMEM((n, d), LOW),
        attended=pltpu.VMEM((n, d), F32),
        resid=pltpu.VMEM((n, d), F32),
        sec=pltpu.VMEM((2 * s.work, d), LOW),
        gm=pltpu.VMEM((2 * s.work, d), LOW),
        act=pltpu.VMEM((2, 2 * s.work, f), LOW),
        gpre=pltpu.VMEM((2, 2 * s.work, f), LOW),
        gs_own=pltpu.VMEM((s.work, d), F32),
        mo_own=pltpu.VMEM((s.work, d), F32),
        gs_out=pltpu.VMEM((s.work, d), LOW),
        mo_out=pltpu.VMEM((s.work, d), LOW),
        gs_in=pltpu.VMEM((s.work, d), LOW),
        mo_in=pltpu.VMEM((s.work, d), LOW),
        spill_out=pltpu.VMEM((4, s.spill, d), LOW),
        spill_in=pltpu.VMEM((5, s.spill, d), LOW),
        mo=pltpu.VMEM((n, d), F32),
        mask_row=pltpu.VMEM((1, s.rows), jnp.int32),
        wanted_row=pltpu.VMEM((1, n), jnp.int32),
        gres=pltpu.VMEM((n, d), F32),
        gfirst=pltpu.VMEM((n, d), F32),
        gatt=pltpu.VMEM((n, d), LOW),
        gmix=pltpu.VMEM((n, d), LOW),
        dqkv=pltpu.VMEM((n, 3 * d), LOW),
        vec=pltpu.VMEM((6, 8, d), F32),
        vec_in=pltpu.VMEM((5, 8, d), F32),
        send_sem=pltpu.SemaphoreType.DMA((112,)),
        recv_sem=pltpu.SemaphoreType.DMA((112,)),
        summed=pltpu.VMEM((2, *s.tail, f), F32),
        router=pltpu.VMEM((d,), LOW),
        one=pltpu.VMEM((d,), LOW),
        two=pltpu.VMEM((d,), LOW),
        write_sem=pltpu.SemaphoreType.DMA((12,)),
        local_sem=pltpu.SemaphoreType.DMA((24,)),
    )
    batch_axes = "bay" if s.folds else ""
    for name, orders, axes, columns in (("m", s.mlp_orders, batch_axes, s.part), ("a", s.att_orders, "dx" + batch_axes, s.pair)):
        for at, order in enumerate(orders):
            left = axes
            found[f"{name}{at}_0"] = pltpu.VMEM(s.table(left, columns), LOW)
            for step, axis in enumerate(order.strip("G")):
                left = left.replace(axis, "")
                found[f"{name}{at}_{step + 1}"] = pltpu.VMEM(s.table(left, columns), LOW)
            if name == "m":
                found[f"u{at}"] = pltpu.VMEM(s.table(axes, columns), LOW)
    if s.folds:
        found["gathered"] = pltpu.VMEM((4, s.pairs, s.block, s.pair), LOW)
    return found


def layer_kernel(s, names, *refs):
    ins, outs, scratch = refs[:12], refs[12:17], refs[17:]
    tokens, cotangent, key_mask, lengths, routed, w_router, gain_one, gain_two, w_qkv, w_out, w_up, w_down = ins
    block_out, o_att, o_vec, grad_tokens, o_mlp = outs
    v = types.SimpleNamespace(**dict(zip(names, scratch, strict=True)), tok=block_out.at[0])
    n, d, f, pair = s.slots, s.width, s.hidden, s.pair
    half_rows = n // 2

    b, m = lax.axis_index("batch"), lax.axis_index("mp")
    lo, hi = m % 2, m // 2
    y = b % 2
    here = {"d": lo, "x": hi, "y": y}
    other_m = {"d": m + 1 - 2 * lo, "x": m + 2 - 4 * hi, "f": 3 - m}
    peer = {axis: (b, to) for axis, to in other_m.items()} | {"y": (b + 1 - 2 * y, m), "q": (b + 1 - 2 * y, other_m["x"])}
    if s.folds:
        zl, zh = (b // 2) % 2, b // 4
        here |= {"a": zl, "b": zh}
        peer |= {"a": (b + 2 - 4 * zl, m), "b": (b + 4 - 8 * zh, m)}

    barrier = pltpu.get_barrier_semaphore()
    for other in peer.values():
        pl.semaphore_signal(barrier, inc=1, device_id=other, device_id_type=MESH)

    sent = []

    def send(src, dst, axis):
        at = len(sent)
        copy = pltpu.make_async_remote_copy(
            src_ref=src,
            dst_ref=dst,
            send_sem=v.send_sem.at[at],
            recv_sem=v.recv_sem.at[at],
            device_id=peer[axis],
            device_id_type=MESH,
        )
        copy.start()
        sent.append(copy)
        return copy

    fetches = []

    def fetch(src, dst):
        fetches.append(pltpu.make_async_copy(src, dst, v.local_sem.at[len(fetches)]))
        fetches[-1].start()
        return fetches[-1]

    writes, stored = [], []

    def write(src, dst):
        writes.append(pltpu.make_async_copy(src, dst, v.write_sem.at[len(writes)]))
        writes[-1].start()

    quarter = s.rows // 4
    quarters = [pl.ds(at * quarter, quarter) for at in range(4)]
    got_wanted = fetch(routed, v.wanted_row)
    got_rows = [fetch(src, dst) for src, dst in ((w_router, v.router), (gain_one, v.one), (gain_two, v.two))]
    got_tok = [fetch(tokens.at[0, there], v.tok.at[there]) for there in quarters]
    got_cot = [fetch(cotangent.at[0, there], v.cot.at[there]) for there in quarters]
    got_mask = fetch(key_mask, v.mask_row)

    got_wanted.wait()
    live_count = lengths[0] // 8
    wanted = jnp.where(iota((1, n), 1) < live_count, v.wanted_row[...], -1).astype(F32)
    on_diagonal = iota((n, n), 0) == iota((n, n), 1)
    wanted_column = jnp.sum(jnp.where(on_diagonal, wanted, 0.0), axis=1, keepdims=True).astype(jnp.int32)
    live = jnp.where(iota((n, 1), 0) < live_count, 1.0, 0.0)
    v.pick[...] = jnp.where(iota((n, s.rows), 1) == wanted_column, 1.0, 0.0).astype(LOW)

    def gather(table, got):
        total = 0.0
        for at in range(4):
            got[at].wait()
            cols = slice(at * quarter, (at + 1) * quarter)
            total = total + mm(v.pick[:, cols], table[cols])
        return total

    picked = gather(v.tok, got_tok)
    v.picked[...] = picked
    for got in got_rows:
        got.wait()
    router_row, one_row, two_row = (row[...].astype(F32).reshape(1, d) for row in (v.router, v.one, v.two))
    gate_rate = 1.0 / (1.0 + jnp.exp(-jnp.sum(picked * router_row, axis=1, keepdims=True)))
    route_gain = live * gate_rate

    got_qkv = fetch(w_qkv, v.wqkv)
    cot_rows = gather(v.cot, got_cot)
    got_out = fetch(w_out, v.wout)
    got_up = fetch(w_up, v.wup.at[0])
    got_down = fetch(w_down, v.wdn.at[0])
    half, work, spill = s.half, s.work, s.spill
    mine_a, other_a = pl.ds(0, half), pl.ds(half, half)
    mine_b, other_b = pl.ds(2 * half, spill), pl.ds(2 * half + spill, spill)
    gm = (route_gain * cot_rows).astype(LOW)
    v.gm[0:half] = gm[:half]
    v.spill_out[0] = gm[work:]

    pl.semaphore_wait(barrier, len(peer))
    sent_gm = [send(v.gm.at[mine_a], v.gm.at[other_a], "x")]
    spilt_gm = send(v.spill_out.at[0], v.spill_in.at[0], "y")
    sent_up = send(w_up, v.wup.at[1], "d")
    sent_down = send(w_down, v.wdn.at[1], "d")

    v.cotr[...] = cot_rows.astype(LOW)
    rate_one = norm_rate(picked)
    v.first[...] = (picked * rate_one * one_row).astype(LOW)
    got_qkv.wait()
    for at in range(0, 3 * d, 256):
        v.qkv[:, at : at + 256] = mm(v.first[...], v.wqkv[:, at : at + 256]).astype(LOW)

    place_spill = jnp.where(iota((spill, spill), 0) + half - live_count == iota((spill, spill), 1), 1.0, 0.0).astype(LOW)
    live_b = live[half:work]

    def merge(own, arrived):
        return (own.astype(F32) * live_b + mm(place_spill, arrived)).astype(LOW)

    def part_back(merged):
        return mm(place_spill, merged, 0, 0).astype(LOW)

    peer_live = 2 * work - live_count
    place_peer = jnp.where(iota((spill, spill), 0) + half - peer_live == iota((spill, spill), 1), 1.0, 0.0).astype(LOW)

    spilt_gm.wait_recv()
    v.gm[2 * half : 2 * half + spill] = merge(gm[half:work], v.spill_in[0])
    sent_gm.append(send(v.gm.at[mine_b], v.gm.at[other_b], "x"))

    got_mask.wait()
    mask_rows = jnp.broadcast_to(v.mask_row[...].astype(F32), (8, s.rows)).astype(LOW)
    key_open = mm(mask_rows, v.pick[...], 1, 1)[0:1] > 0.5
    earlier = iota((n, n), 1) < iota((n, n), 0)
    v.bias[...] = jnp.where((earlier & key_open) | on_diagonal, 0.0, -1e30)

    lane = iota((n, pair), 1)
    side = [lane < pair // 2, lane >= pair // 2]

    def only(x, at):
        return jnp.where(side[at], x.astype(F32), 0.0).astype(LOW)

    for p in range(s.pairs):
        q, k, val = (v.qkv[:, g * d + p * pair : g * d + (p + 1) * pair] for g in range(3))
        q = (q.astype(F32) * (d // HEADS) ** -0.5).astype(LOW)
        total = 0.0
        for h in range(2):
            scores = mm(only(q, h), k, 1, 1) + v.bias[...]
            powers = jnp.exp(scores - jnp.max(scores, axis=1, keepdims=True))
            probs = (powers * (1.0 / jnp.sum(powers, axis=1, keepdims=True))).astype(LOW)
            v.probs[2 * p + h] = probs
            total = total + mm(probs, only(val, h))
        v.mixed[:, p * pair : (p + 1) * pair] = total.astype(LOW)

    got_out.wait()

    def second(start, stop):
        rows = slice(start, stop)
        attended = mm(v.mixed[rows], v.wout[...])
        v.attended[rows] = attended
        resid = v.picked[rows] + attended
        v.resid[rows] = resid
        return (resid * norm_rate(resid) * two_row).astype(LOW)

    normed = second(0, n)
    v.spill_out[1] = normed[work:]
    spilt_sec = send(v.spill_out.at[1], v.spill_in.at[1], "y")
    v.sec[0:half] = normed[:half]
    sent_sec = [send(v.sec.at[mine_a], v.sec.at[other_a], "x")]
    second_b = normed[half:work]

    def feed(start, count):
        rows = slice(start, start + count)
        x, g = v.sec[rows], v.gm[rows]
        gs = 0.0
        for w in range(2):
            act, slope = gelu_and_slope(mm(x, v.wup[w]))
            v.act[w, rows] = act.astype(LOW)
            gpre = (mm(g, v.wdn_t[w]) * slope).astype(LOW)
            v.gpre[w, rows] = gpre
            gs = gs + mm(gpre, v.wup_t[w])
        return gs

    def feed_out(start, count):
        rows = slice(start, start + count)
        return mm(v.act[0, rows], v.wdn[0]) + mm(v.act[1, rows], v.wdn[1])

    got_up.wait()
    got_down.wait()
    sent_up.wait_recv()
    sent_down.wait_recv()
    for w in range(2):
        v.wup_t[w] = v.wup[w].T
        v.wdn_t[w] = v.wdn[w].T
    v.gs_own[0:half] = feed(0, half)
    spilt_sec.wait_recv()
    v.sec[2 * half : 2 * half + spill] = merge(second_b, v.spill_in[1])
    sent_sec.append(send(v.sec.at[mine_b], v.sec.at[other_b], "x"))
    gs = feed(2 * half, spill)
    v.gs_own[half:work] = gs
    v.spill_out[2] = gs.astype(LOW)
    spilt_own = send(v.spill_out.at[2], v.spill_in.at[2], "y")
    v.mo_own[0:half] = feed_out(0, half)
    v.mo_own[half:work] = feed_out(2 * half, spill)
    v.sec_t[:, :half] = v.sec[0:half].T
    v.gm_t[:, :half] = v.gm[0:half].T
    for copy in sent_gm:
        copy.wait_recv()
    v.gm_t[:, half:] = v.gm[half:].T
    sent_gs, sent_mo, spilt = [], [], {}

    def transposes():
        v.wout_t[...] = v.wout[...].T
        v.first_t[...] = v.first[...].T
        v.mixed_t[...] = v.mixed[...].T

    def send_back(out, into, start, count):
        there = pl.ds(start, count)
        return send(out.at[there], into.at[there], "x")

    def feed_other(at):
        sent_sec[at].wait_recv()
        start, count, into = (half, half, 0) if at == 0 else (2 * half + spill, spill, half)
        rows = slice(into, into + count)
        v.gs_out[rows] = feed(start, count).astype(LOW)
        if at == 0:
            sent_gs.append(send_back(v.gs_out, v.gs_in, 0, half // 2))
        else:
            sent_gs.append(send_back(v.gs_out, v.gs_in, half, spill))
            spilt["gs"] = send(v.gs_out.at[pl.ds(half, spill)], v.spill_in.at[4], "q")
            sent_gs.append(send_back(v.gs_out, v.gs_in, half // 2, half // 2))
        v.mo_out[rows] = feed_out(start, count).astype(LOW)
        if at == 1:
            sent_mo.append(send_back(v.mo_out, v.mo_in, half, spill))
            sent_mo.append(send_back(v.mo_out, v.mo_in, 0, half))
            v.sec_t[:, half:] = v.sec[half:].T

    def weight_grad(at, w):
        left, right = (v.sec_t, v.gpre) if at < 3 else (v.gm_t, v.act)
        cols = slice(at % 3 * s.part, (at % 3 + 1) * s.part)
        return mm(left[...], right[w, :, cols])

    sent_core = {}

    def other_core(at):
        table = getattr(v, f"u{at}")
        table[...] = weight_grad(at, 1).astype(LOW).reshape(table.shape)
        sent_core[at] = send(table, getattr(v, f"m{at}_0"), "d")

    class Sum:
        def __init__(self, name, axes, order, finish):
            self.name, self.axes, self.order, self.finish, self.at = name, axes, order, finish, 0
            if order:
                self.start()

        def table(self, at):
            return getattr(v, f"{self.name}_{at}")

        def start(self):
            axis = self.order[self.at]
            src = self.table(self.at).at[tuple(1 - here[k] if k == axis else slice(None) for k in self.axes)]
            self.going = send(src, self.table(self.at + 1), axis)

        def advance(self):
            if self.at == len(self.order):
                self.finish.advance()
                return
            axis = self.order[self.at]
            self.going.wait_recv()
            kept, arrived = self.table(self.at), self.table(self.at + 1)
            last = self.at + 1 == len(self.order)
            rest = self.axes.replace(axis, "")
            for index in itertools.product(*[range(2)] * len(rest)):
                full = dict(zip(rest, index, strict=True)) | {axis: here[axis]}
                total = arrived[index].astype(F32) + kept[tuple(full[k] for k in self.axes)].astype(F32)
                if last:
                    self.finish.begin(total)
                else:
                    arrived[index] = total.astype(LOW)
            self.axes, self.at = rest, self.at + 1
            if not last:
                self.start()

    class Store:
        def __init__(self, at):
            self.at = at

        def begin(self, total):
            kind, cols = self.at // 3, slice(self.at % 3 * s.part, (self.at % 3 + 1) * s.part)
            v.summed[kind, :, cols] = total
            stored.append(self.at)
            if all(3 * kind + at in stored for at in range(3)):
                write(v.summed.at[kind], o_mlp.at[kind])

    class Gather:
        def __init__(self, p, direct):
            self.p, self.direct = p, direct

        def begin(self, total):
            if not s.folds:
                o_att[self.p] = total
                return
            piece = v.gathered.at[m, self.p]
            piece[...] = total.astype(LOW)
            self.over_x = send(piece, piece, "x")
            self.others = [send(piece, piece, "d")]
            if self.direct:
                self.others.append(send(piece, piece, "f"))
            self.handed_on = self.direct

        def advance(self):
            if not self.handed_on:
                self.over_x.wait_recv()
                piece = v.gathered.at[other_m["x"], self.p]
                self.others.append(send(piece, piece, "d"))
                self.handed_on = True
                return
            if self.direct:
                self.over_x.wait_recv()
            for copy in self.others:
                copy.wait_recv()
            for g in range(4):
                o_att[g, self.p] = v.gathered[g, self.p]

    sums = {}

    def own_core(at):
        own = weight_grad(at, 0)
        sent_core[at].wait_recv()
        table = getattr(v, f"m{at}_0")
        table[...] = (table[...].astype(F32) + own.reshape(table.shape)).astype(LOW)
        if s.folds:
            sums[f"m{at}"] = Sum(f"m{at}", "bay", s.mlp_orders[at], Store(at))
        else:
            v.summed[at // 3, :, at % 3 * s.part : (at % 3 + 1) * s.part] = table[...].astype(F32)
            if at % 3 == 2:
                write(v.summed.at[at // 3], o_mlp.at[at // 3])

    gain_two_sums = []

    def second_back(at):
        if at < 3:
            start, stop = ((0, half // 2), (half, work), (half // 2, half))[at]
            sent_gs[at].wait_recv()
            gs = (v.gs_own[start:stop] + v.gs_in[start:stop].astype(F32)).astype(LOW)
            if at == 1:
                gs = gs.astype(F32) * live_b
        else:
            start, stop = work, n
            spilt_own.wait_recv()
            spilt["gs"].wait_recv()
            gs = mm(place_peer, (v.spill_in[2].astype(F32) + v.spill_in[4].astype(F32)).astype(LOW), 0, 0)
        rows = slice(start, stop)
        gs = gs.astype(F32)
        resid = v.resid[rows]
        rate = norm_rate(resid)
        gain_two_sums.append(jnp.sum(gs * (resid * rate), axis=0, keepdims=True))
        scaled = gs * two_row
        gres = rate * scaled - resid * (rate * rate * rate * jnp.mean(scaled * resid, axis=1, keepdims=True))
        v.gres[rows] = gres
        gatt = (route_gain[rows] * v.cotr[rows].astype(F32) + gres).astype(LOW)
        v.gatt[rows] = gatt
        v.gmix[rows] = mm(gatt, v.wout_t[...]).astype(LOW)

    def part_mo(at):
        if at == 0:
            sent_mo[0].wait_recv()
            mo = (v.mo_own[half:work] + v.mo_in[half:work].astype(F32)).astype(LOW)
            v.spill_out[3] = part_back(mo)
            spilt["mo"] = send(v.spill_out.at[3], v.spill_in.at[3], "y")
            v.mo[half:work] = mo.astype(F32)
        else:
            sent_mo[1].wait_recv()
            v.mo[0:half] = (v.mo_own[0:half] + v.mo_in[0:half].astype(F32)).astype(LOW).astype(F32)
            spilt["mo"].wait_recv()
            v.mo[work:n] = v.spill_in[3].astype(F32)

    out_made = []

    def attend_back(p):
        where = [slice(g * d + p * pair, g * d + (p + 1) * pair) for g in range(3)]
        q, k, val = (v.qkv[:, cols] for cols in where)
        gmix = v.gmix[:, p * pair : (p + 1) * pair]
        gq, gk, gv = 0.0, 0.0, 0.0
        for h in range(2):
            probs = v.probs[2 * p + h]
            gmix_h = only(gmix, h)
            gprobs = mm(gmix_h, val, 1, 1)
            wide = probs.astype(F32)
            product = gprobs * wide
            gscores = product - wide * jnp.sum(product, axis=1, keepdims=True)
            gscores = (gscores * (d // HEADS) ** -0.5).astype(LOW)
            gq = gq + mm(gscores, only(k, h))
            gk = gk + mm(gscores, only(q, h), 0, 0)
            gv = gv + mm(probs, gmix_h, 0, 0)
        table = getattr(v, f"a{p}_0")
        lower = []
        for cols, grad in zip(where, (gq, gk, gv), strict=True):
            lower.append(grad.astype(LOW))
            v.dqkv[:, cols] = lower[-1]
        both = mm(v.first_t[...], jnp.concatenate(lower[:2], axis=1)).astype(LOW)
        shape = table.shape[2:]
        table[0, 0] = both[:, :pair].reshape(shape)
        table[1, 0] = both[:, pair:].reshape(shape)
        table[0, 1] = mm(v.first_t[...], lower[2]).astype(LOW).reshape(shape)
        two = p - p % 2
        if two not in out_made:
            out_made.append(two)
            wide = mm(v.mixed_t[...], v.gatt[:, two * pair : (two + 2) * pair]).astype(LOW)
            getattr(v, f"a{two}_0")[1, 1] = wide[:, :pair].reshape(shape)
            getattr(v, f"a{two + 1}_0")[1, 1] = wide[:, pair:].reshape(shape)
        order = s.att_orders[p]
        sums[f"a{p}"] = Sum(f"a{p}", "dxbay" if s.folds else "dx", order.strip("G"), Gather(p, "G" in order))

    kept = {}

    def first_back(at):
        if at == 0:
            v.gfirst[...] = mm(v.dqkv[...], v.wqkv[...], 1, 1)
            return
        gfirst, picked, rate = v.gfirst[...], v.picked[...], rate_one
        kept["gain_one"] = jnp.sum(gfirst * (picked * rate), axis=0, keepdims=True)
        scaled = gfirst * one_row
        gnorm = rate * scaled - picked * (rate * rate * rate * jnp.mean(scaled * picked, axis=1, keepdims=True))
        v.gres[...] = v.gres[...] + gnorm

    def finish_rows():
        picked = v.picked[...]
        branch = v.attended[...] + v.mo[...]
        grate = live * jnp.sum(v.cotr[...].astype(F32) * branch, axis=1, keepdims=True)
        glogit = grate * gate_rate * (1.0 - gate_rate)
        router_sum = jnp.sum(glogit * picked, axis=0, keepdims=True)
        v.upd_out[...] = (route_gain * branch).astype(LOW)
        v.upd_tok[...] = (live * (v.gres[...] + glogit * router_row)).astype(LOW)
        row = iota((8, d), 0)
        gain_two_sum = sum(gain_two_sums)
        v.vec[0] = jnp.where(row == 0, router_sum, jnp.where(row == 1, kept["gain_one"], jnp.where(row == 2, gain_two_sum, 0.0)))
        sums["v"] = Everywhere("dxyab" if s.folds else "dx")

    tile = s.rows // 8

    def spread(at):
        rows = slice(at * tile, (at + 1) * tile)
        there = pl.ds(at * tile, tile)
        place = jnp.where(iota((tile, n), 0) + at * tile == wanted.astype(jnp.int32), 1.0, 0.0).astype(LOW)
        for table, update in ((v.tok, v.upd_out), (v.cot, v.upd_tok)):
            table[rows] = (table[rows].astype(F32) + mm(place, update[...])).astype(LOW)
        write(v.cot.at[there], grad_tokens.at[0, there])

    class Everywhere:
        def __init__(self, order):
            self.order, self.at = order, 0
            self.start()

        def start(self):
            self.going = send(v.vec.at[self.at], v.vec_in.at[self.at], self.order[self.at])

        def advance(self):
            self.going.wait_recv()
            v.vec[self.at + 1] = v.vec[self.at] + v.vec_in[self.at]
            self.at += 1
            if self.at < len(self.order):
                self.start()
            else:
                total = v.vec[self.at]
                if not s.folds:
                    o_vec[...] = total
                    return
                mine = iota((d, s.block), 0) == iota((d, s.block), 1) + b * s.block
                o_vec[...] = lax.dot_general(
                    total, jnp.where(mine, 1.0, 0.0), (((1,), (0,)), ((), ())),
                    preferred_element_type=F32, precision=lax.Precision.HIGHEST,
                )

    steps = {"f": feed_other, "u": other_core, "w": own_core, "r": second_back, "b": attend_back, "s": spread, "o": part_mo, "e": first_back}
    for step in itertools.chain(*SEQUENCE):
        if step[0] in steps:
            steps[step[0]](int(step[1:]))
        elif step == "t":
            transposes()
        elif step == "z":
            finish_rows()
        elif s.folds:
            sums[step].advance()
    if not s.folds:
        for name, total in sums.items():
            total.advance()
            total.advance()
    for copy in sent:
        copy.wait_send()
    for copy in writes:
        copy.wait()


def hand_over_kernel(block_out, att, vec, grad_tokens, mlp, out, tok, g_up, g_down, g_qkv, g_out, *rest):
    vecs, (tok_buf, mlp_buf, qkv_buf, out_buf, *vec_bufs, come_sem, go_sem) = rest[:3], rest[3:]
    _, pairs, _, pair = att.shape
    d = g_out.shape[1]
    rows = tok.shape[1] // 4
    going = []

    def go(src, dst):
        going.append(pltpu.make_async_copy(src, dst, go_sem.at[len(going)]))
        going[-1].start()

    coming = []
    for src, dst in (
        *[(grad_tokens.at[0, pl.ds(at * rows, rows)], tok_buf.at[pl.ds(at * rows, rows)]) for at in range(4)],
        *[(mlp.at[at], mlp_buf.at[at]) for at in range(2)],
    ):
        coming.append(pltpu.make_async_copy(src, dst, come_sem.at[len(coming)]))
        coming[-1].start()
    go(block_out, out)
    for p in range(pairs):
        for g in range(3):
            qkv_buf[:, g * d + p * pair : g * d + (p + 1) * pair] = att[g, p].astype(F32)
        out_buf[:, p * pair : (p + 1) * pair] = att[3, p].astype(F32)
    go(qkv_buf, g_qkv)
    go(out_buf, g_out)
    for at in range(3):
        vec_bufs[at][...] = vec[at : at + 1]
        go(vec_bufs[at], vecs[at])
    for at in range(4):
        coming[at].wait()
        there = pl.ds(at * rows, rows)
        go(tok_buf.at[there], tok.at[0, there])
    for at, dst in enumerate((g_up, g_down)):
        coming[4 + at].wait()
        go(mlp_buf.at[at], dst)
    for copy in going:
        copy.wait()


def hand_over(block_out, att, vec, grad_tokens, mlp):
    _, block, f = mlp.shape
    _, rows, d = block_out.shape
    vmem, hbm, anywhere = (pl.BlockSpec(memory_space=space) for space in (pltpu.VMEM, pltpu.HBM, pl.ANY))
    near = [pltpu.with_memory_space_constraint(x, pltpu.VMEM) for x in (block_out, att, vec)]
    far = [pltpu.with_memory_space_constraint(x, pltpu.HBM) for x in (grad_tokens, mlp)]
    shapes = [((block, f), F32), ((block, f), F32), ((block, 3 * d), F32), ((block, d), F32)]
    return pl.pallas_call(
        hand_over_kernel,
        out_shape=[
            *[jax.ShapeDtypeStruct(block_out.shape, LOW)] * 2,
            *[jax.ShapeDtypeStruct(shape, dtype) for shape, dtype in shapes],
            *[jax.ShapeDtypeStruct((1, block), F32)] * 3,
        ],
        in_specs=[vmem] * 3 + [hbm] * 2,
        out_specs=[anywhere] * 9,
        scratch_shapes=[
            pltpu.VMEM((rows, d), LOW),
            pltpu.VMEM(mlp.shape, F32),
            *[pltpu.VMEM(shape, dtype) for shape, dtype in shapes[2:]],
            *[pltpu.VMEM((1, block), F32)] * 3,
            pltpu.SemaphoreType.DMA((6,)),
            pltpu.SemaphoreType.DMA((12,)),
        ],
        compiler_params=pltpu.CompilerParams(vmem_limit_bytes=16 * 2**20),
        name="hand_over",
    )(*near, *far)


def local(tokens, key_mask, lengths, routed, w_router, gain_one, gain_two, w_qkv, w_out, w_up, w_down, cotangent):
    _, rows, d = tokens.shape
    n, f = routed.shape[1], w_up.shape[1]
    batch = lax.axis_size("batch")
    s = Sizes(rows, d, n, f, batch)
    found = scratch_of(s)
    vmem, smem, anywhere = (pl.BlockSpec(memory_space=space) for space in (pltpu.VMEM, pltpu.SMEM, pl.ANY))
    shape = pltpu.VMEM if s.folds else jax.ShapeDtypeStruct
    block_out, att, vec, grad_tokens, mlp = pl.pallas_call(
        functools.partial(layer_kernel, s, tuple(found)),
        out_shape=(
            shape(tokens.shape, LOW),
            shape((4, s.pairs, s.block, s.pair), LOW) if s.folds else shape((s.pairs, d, s.pair), F32),
            shape((8, s.block if s.folds else d), F32),
            jax.ShapeDtypeStruct(tokens.shape, LOW),
            jax.ShapeDtypeStruct((2, *s.tail, f), F32),
        ),
        in_specs=[anywhere] * 3 + [smem] + [anywhere] * 8,
        out_specs=[vmem] * 3 + [anywhere] * 2,
        scratch_shapes=list(found.values()),
        compiler_params=pltpu.CompilerParams(collective_id=0, has_side_effects=True, vmem_limit_bytes=VMEM_BYTES),
        name="layer",
    )(
        tokens, cotangent, key_mask, lengths, routed, w_router, gain_one, gain_two, w_qkv, w_out, w_up, w_down,
    )
    if s.folds:
        block_out, grad_tokens, g_up, g_down, g_qkv, g_out, *g_vecs = hand_over(block_out, att, vec, grad_tokens, mlp)
    else:
        mlp = lax.psum_scatter(mlp, "batch", scatter_dimension=1, tiled=True)
        vec = lax.psum_scatter(vec, "batch", scatter_dimension=1, tiled=True)
        att = lax.psum_scatter(att, "batch", scatter_dimension=1, tiled=True).astype(LOW)
        att = lax.all_gather(att, "mp", axis=0).astype(F32)
        att = jnp.transpose(att, (2, 0, 1, 3)).reshape(s.block, 4 * d)
        (g_up, g_down), g_qkv, g_out, g_vecs = mlp, att[:, : 3 * d], att[:, 3 * d :], vec[:3]
    g_router, g_one, g_two = (g.reshape(s.block) for g in g_vecs)
    return block_out, grad_tokens, g_router, g_one, g_two, g_qkv, g_out, g_up, g_down.T


def solution(mesh):
    rows_spec = P(("batch", "mp"), None, None)
    in_specs = (
        rows_spec,
        P(("batch", "mp"), None),
        P(("batch", "mp")),
        P(("batch", "mp"), None),
        P(),
        P(),
        P(),
        P(),
        P(),
        P(None, "mp"),
        P("mp", None),
        rows_spec,
    )
    out_specs = (
        rows_spec,
        rows_spec,
        P("batch"),
        P("batch"),
        P("batch"),
        P("batch", None),
        P("batch", None),
        P("batch", "mp"),
        P("mp", "batch"),
    )
    return jax.shard_map(local, mesh=mesh, in_specs=in_specs, out_specs=out_specs, check_vma=False)
```
